1024 devices in a mesh: table: 64 (over z, core), cuts: 16 (over x, y).
Axes of the slice: x: 4, y: 4, z: 32, core: 2. Of those that a mesh axis runs over, the one named last changes fastest.
Arguments:
- embedding: bfloat16 [1048576, 128], P('table', 'cuts'), may hold values from -6 to 6
- cross_weight: bfloat16 [4096, 4096], P(None, 'cuts'), may hold values from -0.09375 to 0.09375
- cross_bias: float32 [4096], P('cuts'), may hold values from -5 to 5
- upstream: bfloat16 [8192, 4096], P('table', 'cuts'), may hold values from -6 to 6
- unique_rows: int32 [64, 64, 16], P(None, 'table'), may hold values from 0 to 16383, as said below
- lookup_slot: int32 [64, 8192], P('table'), may hold values from 0 to 1023, as said below
- bag_of_lookup: int32 [64, 8192], P('table'), may hold values from 0 to 4095, never falling along the last dimension, each value on 1 to 8 neighbouring positions
Outputs:
- cross_out: bfloat16 [8192, 4096], P('table', 'cuts')
- row_grads: float32 [1048576, 128], P('table', 'cuts')
The draws below stay inside these ranges and needn't reach their ends.
Inputs may be any that keep to these rules, and one draw needn't show every extreme that they name: For each s and p the 16 entries unique_rows[s, p, :] are distinct local rows of owner p. lookup_slot[s, l] = p * 16 + j names slot j of shard s's request list to owner p.
All inputs are finite; a program needn't handle non-finite values.
Results may differ from the reference program's by a relative error of at most 0.0095.
Values may be sent and summed in bfloat16 or wider, within the bound.
No kernel may reach another device: no remote copies, remote signals or barrier semaphores. Data moves between devices by JAX's collectives and lax.ppermute only.
A program may use at most 64 MiB of HBM per device.

```python
import math
import jax
import jax.numpy as jnp
import numpy as np
from jax import lax

EMB = 128
F = 32
B_DEV = 128
CAP = 16
ROWS_DEV = 16384
WIDTH = 4096
LOOK_DEV = 8192
SHARDS = 64
SAMPLES = 8192
TOTAL_ROWS = 1048576
N_CUTS = 16


def slot_counts(key):
    hot_key, low_key = jax.random.split(key)
    order = jax.random.permutation(hot_key, SHARDS)
    last_owner = jnp.arange(SHARDS, dtype=jnp.int32) == SHARDS - 1
    hot_owner = (order < max(SHARDS // 16, 1)) | last_owner
    low_counts = jax.random.randint(low_key, (SHARDS, SHARDS), max(CAP // 4, 1), CAP // 2 + 1)
    return jnp.where(hot_owner[None, :], CAP, low_counts).astype(jnp.int32)


def draw_unique_rows(key, part):
    key = jax.random.fold_in(key, 11)
    offset_key, shift_key = jax.random.split(key)
    stride = ROWS_DEV // CAP
    offsets = jax.random.randint(offset_key, (SHARDS, SHARDS, CAP), 0, stride)
    shifts = jax.random.randint(shift_key, (SHARDS, SHARDS, 1), 0, CAP)
    bucket = (jnp.arange(CAP, dtype=jnp.int32)[None, None, :] + shifts) % CAP
    return (bucket * stride + offsets).astype(jnp.int32)


def draw_lookup_slot(key, part):
    counts = slot_counts(key)
    key = jax.random.fold_in(key, 23)
    owner_key, slot_key = jax.random.split(key)
    owner = jax.random.randint(owner_key, (SHARDS, LOOK_DEV), 0, SHARDS)
    limit = jnp.take_along_axis(counts, owner, axis=1)
    within = jax.random.randint(slot_key, (SHARDS, LOOK_DEV), 0, limit)
    slots = (owner * CAP + within).astype(jnp.int32)
    position = jnp.arange(LOOK_DEV, dtype=jnp.int32)[None, :]
    slots = jnp.where(position == 0, 0, slots)
    slots = jnp.where(position == LOOK_DEV - 1, SHARDS * CAP - 1, slots)
    return slots.astype(jnp.int32)


def levels(key, dims, shards, smallest, largest):
    def one(dim, blocks):
        draws = jax.random.uniform(jax.random.fold_in(jax.random.fold_in(key, 6), dim), (blocks,), jnp.float32, smallest / len(shards), largest / len(shards))
        return jnp.repeat(jnp.exp(draws), dims[dim] // blocks).reshape((-1,) + (1,) * (len(dims) - dim - 1))

    level = one(*shards[0])
    for cut in shards[1:]:
        level = level * one(*cut)
    return level


def split_up(number_of, total, reach, lean):
    portions = [(1 << 20) // math.isqrt(standing ** lean) + 1 for standing in range(2, number_of + 1)]
    spare, given = total - reach - (number_of - 1), [1] * (number_of - 1)
    while spare > 0:
        candidates = [i for i in range(number_of - 1) if given[i] < reach]
        whole, budget = sum([portions[i] for i in candidates]), spare
        for i in candidates:
            extra = min(reach - given[i], max(1, budget * portions[i] // whole), spare)
            given[i] = given[i] + extra
            spare = spare - extra
    return np.array([reach] + given)


def uneven(stream_key, count, total, most, skew):
    if count == 2:
        one = jax.random.randint(stream_key, (), max(1, total - most), min(most, total - 1) + 1)
        return jnp.stack([one, total - one])
    sizes = jnp.asarray(split_up(count, total, most, skew), jnp.int32)
    pairs = (count - 1) // 2
    giver, sink = sizes[1:1 + 2 * pairs:2], sizes[2:2 + 2 * pairs:2]
    room = jnp.minimum(giver - 1, most - sink)
    passed = jax.random.randint(jax.random.fold_in(stream_key, 1), (pairs,), 0, 1 << 20) % (room + 1)
    sizes = sizes.at[1:1 + 2 * pairs:2].set(giver - passed).at[2:2 + 2 * pairs:2].set(sink + passed)
    return sizes[jax.random.permutation(jax.random.fold_in(stream_key, 2), count)]


def scatter_about(key, shape, deviation, most, cuts=(), kind=jnp.bfloat16):
    drawn = jax.random.normal(key, shape, jnp.float32) * deviation
    if len(cuts) > 0:
        drawn = levels(key, shape, cuts, -0.22, 0.18) * drawn
    return jnp.clip(drawn, min=-most, max=most).astype(kind)


def setup_inputs(seed: int = 0) -> dict:
    arg_keys = jax.random.split(jax.random.key(seed), 8)
    embedding = scatter_about(arg_keys[0], (TOTAL_ROWS, EMB), 1.0, 6.0, ((0, 64), (1, 16)))
    cross_weight = scatter_about(arg_keys[1], (WIDTH, WIDTH), WIDTH ** -0.5, 0.09375, ((1, 16),))
    cross_bias = scatter_about(arg_keys[2], (WIDTH,), 1.0, 5.0, ((0, 16),), jnp.float32)
    upstream = scatter_about(arg_keys[3], (SAMPLES, WIDTH), 1.0, 6.0, ((0, 64), (1, 16)))
    unique_rows = draw_unique_rows(jax.random.fold_in(arg_keys[7], 71), 0)
    lookup_slot = draw_lookup_slot(jax.random.fold_in(arg_keys[7], 71), 0)
    bag_of_lookup = jax.vmap(lambda own: jnp.searchsorted(jnp.cumsum(uneven(own, B_DEV * F, LOOK_DEV, 8, 2)), jnp.arange(LOOK_DEV), side="right"))(jax.random.split(arg_keys[6], SHARDS)).reshape((SHARDS, LOOK_DEV)).astype(jnp.int32)
    return {"embedding": embedding, "cross_weight": cross_weight, "cross_bias": cross_bias, "upstream": upstream, "unique_rows": unique_rows, "lookup_slot": lookup_slot, "bag_of_lookup": bag_of_lookup}


def shard_step(cross_weight, cross_bias, inputs):
    rows_here, slot_index, bag_index, grad_above = inputs
    width_cols = EMB // N_CUTS
    looked = jnp.take(rows_here, slot_index, axis=0).astype(jnp.float32)
    pooled = jax.ops.segment_sum(looked, bag_index, num_segments=B_DEV * F, indices_are_sorted=True).astype(jnp.bfloat16)
    base = pooled.reshape(B_DEV, F, N_CUTS, width_cols).transpose(0, 2, 1, 3).reshape(B_DEV, WIDTH)
    mix = jnp.dot(base, cross_weight, preferred_element_type=jnp.float32) + cross_bias
    base_wide = base.astype(jnp.float32)
    cross_out = (base_wide * mix + base_wide).astype(jnp.bfloat16)
    grad_wide = grad_above.astype(jnp.float32)
    mix_grad = (grad_wide * base_wide).astype(jnp.bfloat16)
    base_grad = grad_wide * (mix + 1.0) + jnp.dot(mix_grad, cross_weight.T, preferred_element_type=jnp.float32)
    bag_grad = base_grad.reshape(B_DEV, N_CUTS, F, width_cols).transpose(0, 2, 1, 3).reshape(B_DEV * F, EMB)
    per_lookup = jnp.take(bag_grad, bag_index, axis=0)
    slot_grad = jax.ops.segment_sum(per_lookup, slot_index, num_segments=SHARDS * CAP)
    return cross_out, slot_grad


def reference(embedding, cross_weight, cross_bias, upstream, unique_rows, lookup_slot, bag_of_lookup):
    stacked = embedding.reshape(SHARDS, ROWS_DEV, EMB)
    owners = jnp.arange(SHARDS, dtype=jnp.int32)[None, :, None]
    requested = stacked[owners, unique_rows]
    requested = requested.reshape(SHARDS, SHARDS * CAP, EMB)
    grads_split = upstream.reshape(SHARDS, B_DEV, WIDTH)
    cross_out, slot_grad = lax.map(partial_step(cross_weight, cross_bias), (requested, lookup_slot, bag_of_lookup, grads_split))
    slot_grad = slot_grad.reshape(SHARDS, SHARDS, CAP, EMB)
    row_grads = jnp.zeros((SHARDS, ROWS_DEV, EMB), jnp.float32).at[owners, unique_rows].add(slot_grad)
    return cross_out.reshape(SAMPLES, WIDTH), row_grads.reshape(TOTAL_ROWS, EMB)


def partial_step(cross_weight, cross_bias):
    def apply_step(inputs):
        return shard_step(cross_weight, cross_bias, inputs)
    return apply_step
```

```python
import functools

import jax
import jax.numpy as jnp
from jax import lax
from jax.experimental import pallas as pl
from jax.experimental.pallas import tpu as pltpu
from jax.sharding import PartitionSpec as P

LANES = 128
LOOK_BLOCK = 256
WINDOW = LOOK_BLOCK + 8
NT = (((1,), (1,)), ((), ()))


def dot(a, b):
    return jnp.dot(a, b, preferred_element_type=jnp.float32)


def dot_nt(a, b):
    return lax.dot_general(a, b, NT, preferred_element_type=jnp.float32)


def swap_blocks(parts, width):
    parts = list(parts)
    count = len(parts)
    lanes = parts[0].shape[1]
    block = lax.broadcasted_iota(jnp.int32, parts[0].shape, 1) // width
    step = 1
    while step < count:
        high = (block & step) != 0
        for a in range(count):
            if a & step:
                continue
            low_part, high_part = parts[a], parts[a | step]
            parts[a] = jnp.where(high, pltpu.roll(high_part, step * width, 1), low_part)
            parts[a | step] = jnp.where(
                high, high_part, pltpu.roll(low_part, lanes - step * width, 1)
            )
        step *= 2
    return parts


def row_halves(ids_ref, group, per):
    ids = jnp.concatenate([ids_ref[group * per + k : group * per + k + 1, :] for k in range(per)], axis=1)
    return ids // LANES, ids % LANES


def pick_kernel(ids_ref, emb_ref, out_ref):
    cap, shards = ids_ref.shape
    columns = out_ref.shape[1] // cap
    highs = emb_ref.shape[0] // columns
    per = 256 // shards
    pieces = []
    for group in range(cap // per):
        hi, lo = row_halves(ids_ref, group, per)
        n = hi.shape[1]
        low_hot = (lax.broadcasted_iota(jnp.int32, (LANES, n), 0) == lo).astype(jnp.float32).astype(jnp.bfloat16)
        wide = dot(emb_ref[...], low_hot).reshape(highs, columns, n)
        high_hot = lax.broadcasted_iota(jnp.int32, (highs, columns, n), 0) == hi[None]
        found = jnp.sum(jnp.where(high_hot, wide, 0.0), axis=0)
        for k in range(per):
            pieces.append(found[:, k * shards : (k + 1) * shards])
    out_ref[...] = jnp.concatenate(pieces, axis=0).T.astype(out_ref.dtype)


def scatter_kernel(ids_ref, grad_ref, out_ref):
    cap, shards = ids_ref.shape
    columns = grad_ref.shape[1] // cap
    highs = out_ref.shape[0] // columns
    per = 256 // shards
    turned = grad_ref[...].astype(jnp.float32).T
    for group in range(cap // per):
        hi, lo = row_halves(ids_ref, group, per)
        n = hi.shape[1]
        low_hot = (lax.broadcasted_iota(jnp.int32, (LANES, n), 0) == lo).astype(jnp.float32).astype(jnp.bfloat16)
        values = jnp.concatenate(
            [turned[(group * per + k) * columns : (group * per + k + 1) * columns] for k in range(per)],
            axis=1,
        )
        high_hot = lax.broadcasted_iota(jnp.int32, (highs, columns, n), 0) == hi[None]
        spread = jnp.where(high_hot, values[None], 0.0).reshape(highs * columns, n).astype(jnp.bfloat16)
        part = dot_nt(spread, low_hot)
        if group == 0:
            out_ref[...] = part
        else:
            out_ref[...] += part


def count_kernel(cap, tables, firsts_ref, slot_ref, bag_ref, out_ref, acc):
    look = slot_ref.shape[1]
    slots = out_ref.shape[1]
    owners = slots // cap
    batch = out_ref.shape[0] // tables
    for n in range(slots // LANES):
        acc[n, 0:8, :] = jnp.zeros((8, LANES), jnp.float32)

    def body(i, carry):
        at = pl.ds(pl.multiple_of(i * LOOK_BLOCK, LOOK_BLOCK), LOOK_BLOCK)
        start = pl.multiple_of(firsts_ref[0, i * LOOK_BLOCK] // 8 * 8, 8)
        bags = bag_ref[:, at] - start
        slot = slot_ref[:, at]
        order = slot % cap * owners + slot // cap
        bag_hot = (lax.broadcasted_iota(jnp.int32, (WINDOW, LOOK_BLOCK), 0) == bags).astype(jnp.float32).astype(jnp.bfloat16)
        for n in range(slots // 256):
            slot_hot = (
                (lax.broadcasted_iota(jnp.int32, (256, LOOK_BLOCK), 0) + n * 256 == order)
                .astype(jnp.float32)
                .astype(jnp.bfloat16)
            )
            part = dot_nt(bag_hot, slot_hot)
            for m in range(2):
                cols = slice(m * LANES, (m + 1) * LANES)
                acc[2 * n + m, pl.ds(start, 8), :] += part[0:8, cols]
                acc[2 * n + m, pl.ds(start + 8, WINDOW - 8), :] = part[8:, cols]
        return carry

    lax.fori_loop(0, look // LOOK_BLOCK, body, 0)
    for f in range(tables):
        row = (f % 2 * (tables // 2) + f // 2) * batch
        for n in range(slots // LANES):
            cols = slice(n * LANES, (n + 1) * LANES)
            out_ref[row : row + batch, cols] = acc[n, pl.ds(f, batch, stride=tables), :].astype(jnp.bfloat16)


def cross_kernel(cap, own_ref, rows_ref, count_ref, weight_ref, bias_ref, up_ref, out_ref, grad_ref, base_s, turned_s):
    cuts, owners, lanes = rows_ref.shape
    columns = lanes // cap
    batch, share = up_ref.shape
    pairs = share // (2 * columns)
    own = own_ref[0]

    picked = swap_blocks([rows_ref[q].astype(jnp.float32) for q in range(cuts)], columns)
    rows = jnp.concatenate(picked, axis=0).astype(jnp.bfloat16)
    wide = 2 * lanes
    r = lax.broadcasted_iota(jnp.int32, (lanes, wide), 0)
    l = lax.broadcasted_iota(jnp.int32, (lanes, wide), 1)
    same = (l // (2 * columns) == r // columns) & (l % columns == r % columns)
    odd = (l // columns) % 2 == 1
    put_even = jnp.where(same & ~odd, 1.0, 0.0).astype(jnp.bfloat16)
    put_odd = jnp.where(same & odd, 1.0, 0.0).astype(jnp.bfloat16)
    rows_even = dot(rows, put_even).astype(jnp.bfloat16)
    rows_odd = dot(rows, put_odd).astype(jnp.bfloat16)

    half = pairs * batch
    chunk = 4 * batch
    for c in range(half // chunk):
        at = c * chunk
        both = dot(count_ref[at : at + chunk, :], rows_even) + dot(
            count_ref[half + at : half + at + chunk, :], rows_odd
        )
        base_s[at : at + chunk, :] = both.astype(jnp.bfloat16)

    lane_block = lax.broadcasted_iota(jnp.int32, (batch, lanes), 1) // (2 * columns)
    per_half = lanes // (2 * columns)
    mix = jnp.zeros((batch, share), jnp.float32)
    own_base = [jnp.zeros((batch, lanes), jnp.float32) for _ in range(2)]
    weights = []
    for pair in range(pairs):
        base = base_s[pair * batch : (pair + 1) * batch, :]
        weight = jnp.concatenate(
            [
                weight_ref[q * share + pair * 2 * columns : q * share + (pair + 1) * 2 * columns, :]
                for q in range(cuts)
            ],
            axis=0,
        )
        mix = mix + dot(base, weight)
        mine = jnp.where(own < cuts // 2, base[:, :lanes].astype(jnp.float32), base[:, lanes:].astype(jnp.float32))
        shift = (pair % per_half - own % per_half + per_half) % per_half * (2 * columns)
        moved = pltpu.roll(mine, shift, 1)
        side = pair // per_half
        own_base[side] = jnp.where(lane_block == pair % per_half, moved, own_base[side])
    base_wide = jnp.concatenate(own_base, axis=1)
    mix = mix + bias_ref[...]
    out_ref[...] = (base_wide * mix + base_wide).astype(jnp.bfloat16)
    up = up_ref[...].astype(jnp.float32)
    mix_grad = (up * base_wide).astype(jnp.bfloat16)
    local = (up * (mix + 1.0)).T

    q_index = lax.broadcasted_iota(jnp.int32, (cuts, 2 * columns, batch), 0)
    for pair in range(pairs):
        weight = jnp.concatenate(
            [
                weight_ref[q * share + pair * 2 * columns : q * share + (pair + 1) * 2 * columns, :]
                for q in range(cuts)
            ],
            axis=0,
        )
        back = dot_nt(weight, mix_grad).reshape(cuts, 2 * columns, batch)
        term = local[pair * 2 * columns : (pair + 1) * 2 * columns]
        back = back + jnp.where(q_index == own, term[None], 0.0)
        at = pair * batch
        turned_s[:, at : at + batch] = back[:, :columns].reshape(lanes, batch).astype(jnp.bfloat16)
        turned_s[:, half + at : half + at + batch] = back[:, columns:].reshape(lanes, batch).astype(jnp.bfloat16)
    slot_grad = dot(turned_s[...], count_ref[...]).T
    parts = swap_blocks([slot_grad[j * owners : (j + 1) * owners] for j in range(cap)], columns)
    for q in range(cuts):
        grad_ref[q] = parts[q].astype(jnp.bfloat16)


def call(kernel, out_shape, in_spaces, scratch=(), limit=48, **kw):
    outs = jax.tree.map(lambda unused: pl.BlockSpec(memory_space=pltpu.VMEM), out_shape)
    return pl.pallas_call(
        kernel,
        out_shape=out_shape,
        in_specs=[pl.BlockSpec(memory_space=space) for space in in_spaces],
        out_specs=outs,
        scratch_shapes=list(scratch),
        compiler_params=pltpu.CompilerParams(vmem_limit_bytes=limit * 2**20),
        **kw,
    )


def pick(ids, emb, shards, lanes, **kw):
    V = pltpu.VMEM
    return call(pick_kernel, jax.ShapeDtypeStruct((shards, lanes), jnp.bfloat16), [V, V], **kw)(ids, emb)


def scatter(ids, grads, rows_out, **kw):
    V = pltpu.VMEM
    return call(scatter_kernel, jax.ShapeDtypeStruct((rows_out, LANES), jnp.float32), [V, V], **kw)(ids, grads)


def count(slot, bag, cap, tables, bags, slots, **kw):
    V, S = pltpu.VMEM, pltpu.SMEM
    return call(
        functools.partial(count_kernel, cap, tables),
        jax.ShapeDtypeStruct((bags, slots), jnp.bfloat16),
        [S, V, V],
        [pltpu.VMEM((slots // LANES, bags + WINDOW, LANES), jnp.float32)],
        **kw,
    )(bag, slot, bag)


def cross(own, rows, counts, weight, bias, up, cap, **kw):
    V, S = pltpu.VMEM, pltpu.SMEM
    cuts, owners, lanes = rows.shape
    batch, share = up.shape
    return call(
        functools.partial(cross_kernel, cap),
        (jax.ShapeDtypeStruct(up.shape, jnp.bfloat16), jax.ShapeDtypeStruct(rows.shape, jnp.bfloat16)),
        [S, V, V, V, V, V],
        [
            pltpu.VMEM((counts.shape[0] // 2, 2 * lanes), jnp.bfloat16),
            pltpu.VMEM((lanes, counts.shape[0]), jnp.bfloat16),
        ],
        **kw,
    )(own, rows, counts, weight, bias, up)


def per_device(embedding, cross_weight, cross_bias, upstream, unique_rows, lookup_slot, bag_of_lookup):
    owners = lax.axis_size("table")
    cuts = lax.axis_size("cuts")
    rows_dev, columns = embedding.shape
    cap = unique_rows.shape[2]
    batch, share = upstream.shape
    tables = share // columns
    lanes = cap * columns
    highs = rows_dev // LANES
    ids = unique_rows[:, 0, :].T
    emb = embedding.T.reshape(columns, highs, LANES).transpose(1, 0, 2).reshape(highs * columns, LANES)
    picked = pick(ids, emb, owners, lanes)
    arrived = lax.all_to_all(picked, "table", 0, 0, tiled=True)
    counts = count(lookup_slot, bag_of_lookup, cap, tables, batch * tables, owners * cap)
    rows = lax.all_to_all(
        jnp.broadcast_to(arrived[None], (cuts,) + arrived.shape), "cuts", 0, 0, tiled=True
    )
    own = lax.axis_index("cuts").astype(jnp.int32).reshape(1)
    cross_out, grads = cross(own, rows, counts, cross_weight, cross_bias.reshape(1, share), upstream, cap)
    grads = lax.all_to_all(grads, "cuts", 0, 0, tiled=True)
    grads = jnp.sum(grads.astype(jnp.float32), axis=0).astype(jnp.bfloat16)
    returned = lax.all_to_all(grads, "table", 0, 0, tiled=True)
    row_grads = scatter(ids, returned, highs * columns)
    row_grads = row_grads.reshape(highs, columns, LANES).transpose(1, 0, 2).reshape(columns, rows_dev).T
    return cross_out, row_grads


def solution(mesh):
    return jax.shard_map(
        per_device,
        mesh=mesh,
        in_specs=(
            P("table", "cuts"),
            P(None, "cuts"),
            P("cuts"),
            P("table", "cuts"),
            P(None, "table", None),
            P("table", None),
            P("table", None),
        ),
        out_specs=(P("table", "cuts"), P("table", "cuts")),
        check_vma=False,
    )
```

```python
import functools

import jax
import jax.numpy as jnp
from jax import lax
from jax.experimental import pallas as pl
from jax.experimental.pallas import tpu as pltpu
from jax.sharding import PartitionSpec as P

LANES = 128
LOOK_BLOCK = 256
NT = (((1,), (1,)), ((), ()))


def dot(a, b):
    return jnp.dot(a, b, preferred_element_type=jnp.float32)


def dot_nt(a, b):
    return lax.dot_general(a, b, NT, preferred_element_type=jnp.float32)


def one_hot(hit):
    return hit.astype(jnp.float32).astype(jnp.bfloat16)


def window_rows(tables, pitch):
    return (LOOK_BLOCK + 7 + (LOOK_BLOCK // tables + 1) * (pitch - tables) + 7) // 8 * 8


def swap_blocks(parts, width):
    parts = list(parts)
    count = len(parts)
    lanes = parts[0].shape[1]
    block = lax.broadcasted_iota(jnp.int32, parts[0].shape, 1) // width
    step = 1
    while step < count:
        high = (block & step) != 0
        for a in range(count):
            if a & step:
                continue
            low_part, high_part = parts[a], parts[a | step]
            parts[a] = jnp.where(high, pltpu.roll(high_part, step * width, 1), low_part)
            parts[a | step] = jnp.where(
                high, high_part, pltpu.roll(low_part, lanes - step * width, 1)
            )
        step *= 2
    return parts


def row_halves(ids_ref, group, per):
    ids = jnp.concatenate([ids_ref[group * per + k : group * per + k + 1, :] for k in range(per)], axis=1)
    return ids // LANES, ids % LANES


def pick_kernel(ids_hbm, emb_hbm, out_ref, ids_ref, emb_ref, ids_sem, emb_sem):
    emb_copy = pltpu.make_async_copy(emb_hbm, emb_ref, emb_sem)
    ids_copy = pltpu.make_async_copy(ids_hbm, ids_ref, ids_sem)
    emb_copy.start()
    ids_copy.start()
    ids_copy.wait()
    emb_copy.wait()
    cap, shards = ids_ref.shape
    columns = out_ref.shape[1] // cap
    highs = emb_ref.shape[0] // columns
    per = 256 // shards
    pieces = []
    for group in range(cap // per):
        hi, lo = row_halves(ids_ref, group, per)
        n = hi.shape[1]
        low_hot = one_hot(lax.broadcasted_iota(jnp.int32, (LANES, n), 0) == lo)
        wide = dot(emb_ref[...], low_hot).reshape(highs, columns, n)
        high_hot = lax.broadcasted_iota(jnp.int32, (highs, columns, n), 0) == hi[None]
        found = jnp.sum(jnp.where(high_hot, wide, 0.0), axis=0)
        for k in range(per):
            pieces.append(found[:, k * shards : (k + 1) * shards])
    out_ref[...] = jnp.concatenate(pieces, axis=0).T.astype(out_ref.dtype)


def scatter_kernel(ids_ref, grad_ref, out_ref):
    cap, shards = ids_ref.shape
    columns = grad_ref.shape[1] // cap
    highs = out_ref.shape[0] // columns
    per = 256 // shards
    turned = grad_ref[...].astype(jnp.float32).T
    for group in range(cap // per):
        hi, lo = row_halves(ids_ref, group, per)
        n = hi.shape[1]
        low_hot = one_hot(lax.broadcasted_iota(jnp.int32, (LANES, n), 0) == lo)
        values = jnp.concatenate(
            [turned[(group * per + k) * columns : (group * per + k + 1) * columns] for k in range(per)],
            axis=1,
        )
        high_hot = lax.broadcasted_iota(jnp.int32, (highs, columns, n), 0) == hi[None]
        spread = jnp.where(high_hot, values[None], 0.0).reshape(highs * columns, n).astype(jnp.bfloat16)
        part = dot_nt(spread, low_hot)
        if group == 0:
            out_ref[...] = part
        else:
            out_ref[...] += part


def count_kernel(cap, owners, tables, pitch, first_slot, firsts_ref, slot_ref, bag_ref, out_hbm, acc, out_ref, sems):
    look = slot_ref.shape[1]
    slots = out_ref.shape[1]
    batch = out_ref.shape[0] // tables
    gap = pitch - tables
    window = window_rows(tables, pitch)
    for n in range(slots // LANES):
        acc[n, 0:8, :] = jnp.zeros((8, LANES), jnp.float32)

    def body(i, carry):
        at = pl.ds(pl.multiple_of(i * LOOK_BLOCK, LOOK_BLOCK), LOOK_BLOCK)
        first = firsts_ref[0, i * LOOK_BLOCK]
        start = pl.multiple_of((first + first // tables * gap) // 8 * 8, 8)
        bags = bag_ref[:, at]
        bags = bags + bags // tables * gap - start
        slot = slot_ref[:, at]
        order = slot % cap * owners + slot // cap - first_slot
        bag_hot = one_hot(lax.broadcasted_iota(jnp.int32, (window, LOOK_BLOCK), 0) == bags)
        for n in range(slots // 256):
            slot_hot = one_hot(lax.broadcasted_iota(jnp.int32, (256, LOOK_BLOCK), 0) + n * 256 == order)
            part = dot_nt(bag_hot, slot_hot)
            for m in range(2):
                cols = slice(m * LANES, (m + 1) * LANES)
                acc[2 * n + m, pl.ds(start, 8), :] += part[0:8, cols]
                acc[2 * n + m, pl.ds(start + 8, window - 8), :] = part[8:, cols]
        return carry

    lax.fori_loop(0, look // LOOK_BLOCK, body, 0, unroll=4)
    chunks = sems.shape[0]
    copies = []
    for place in range(tables):
        half = tables // 2
        f = place % half * 2 + place // half
        row = place * batch
        for n in range(slots // LANES):
            cols = slice(n * LANES, (n + 1) * LANES)
            out_ref[row : row + batch, cols] = acc[n, pl.ds(f, batch, stride=pitch), :].astype(jnp.bfloat16)
        if (place + 1) % (tables // chunks) == 0:
            done = pl.ds(len(copies) * (out_ref.shape[0] // chunks), out_ref.shape[0] // chunks)
            copies.append(pltpu.make_async_copy(out_ref.at[done], out_hbm.at[done], sems.at[len(copies)]))
            copies[-1].start()
    for copy in copies:
        copy.wait()


def cross_kernel(
    cap, own_ref, rows_ref, low_hbm, high_hbm, weight_ref, bias_ref, up_ref, out_ref, grad_ref,
    count_ref, base_s, turned_s, sems,
):
    cuts, owners, lanes = rows_ref.shape
    columns = lanes // cap
    batch, share = up_ref.shape
    pairs = share // (2 * columns)
    own = own_ref[0]
    half = pairs * batch
    chunk = 4 * batch
    width = low_hbm.shape[1]
    copies = []
    for c in range(half // chunk):
        for k, (source, at, left) in enumerate(
            (source, side + c * chunk, left)
            for side in (0, half)
            for source, left in ((low_hbm, 0), (high_hbm, width))
        ):
            copies.append(
                pltpu.make_async_copy(
                    source.at[pl.ds(at, chunk)],
                    count_ref.at[pl.ds(at, chunk), pl.ds(left, width)],
                    sems.at[c * 4 + k],
                )
            )
            copies[-1].start()

    picked = swap_blocks([rows_ref[q].astype(jnp.float32) for q in range(cuts)], columns)
    rows = jnp.concatenate(picked, axis=0).astype(jnp.bfloat16)
    wide = 2 * lanes
    r = lax.broadcasted_iota(jnp.int32, (lanes, wide), 0)
    l = lax.broadcasted_iota(jnp.int32, (lanes, wide), 1)
    same = (l // (2 * columns) == r // columns) & (l % columns == r % columns)
    odd = (l // columns) % 2 == 1
    put_even = jnp.where(same & ~odd, 1.0, 0.0).astype(jnp.bfloat16)
    put_odd = jnp.where(same & odd, 1.0, 0.0).astype(jnp.bfloat16)
    rows_even = dot(rows, put_even).astype(jnp.bfloat16)
    rows_odd = dot(rows, put_odd).astype(jnp.bfloat16)

    for c in range(half // chunk):
        at = c * chunk
        for copy in copies[c * 4 : c * 4 + 4]:
            copy.wait()
        both = dot(count_ref[at : at + chunk, :], rows_even) + dot(
            count_ref[half + at : half + at + chunk, :], rows_odd
        )
        base_s[at : at + chunk, :] = both.astype(jnp.bfloat16)

    lane_block = lax.broadcasted_iota(jnp.int32, (batch, lanes), 1) // (2 * columns)
    per_half = lanes // (2 * columns)
    mix = jnp.zeros((batch, share), jnp.float32)
    own_base = [jnp.zeros((batch, lanes), jnp.float32) for _ in range(2)]
    weights = []
    for pair in range(pairs):
        base = base_s[pair * batch : (pair + 1) * batch, :]
        weight = jnp.concatenate(
            [
                weight_ref[q * share + pair * 2 * columns : q * share + (pair + 1) * 2 * columns, :]
                for q in range(cuts)
            ],
            axis=0,
        )
        mix = mix + dot(base, weight)
        mine = jnp.where(own < cuts // 2, base[:, :lanes].astype(jnp.float32), base[:, lanes:].astype(jnp.float32))
        shift = (pair % per_half - own % per_half + per_half) % per_half * (2 * columns)
        moved = pltpu.roll(mine, shift, 1)
        side = pair // per_half
        own_base[side] = jnp.where(lane_block == pair % per_half, moved, own_base[side])
    base_wide = jnp.concatenate(own_base, axis=1)
    mix = mix + bias_ref[...]
    out_ref[...] = (base_wide * mix + base_wide).astype(jnp.bfloat16)
    up = up_ref[...].astype(jnp.float32)
    mix_grad = (up * base_wide).astype(jnp.bfloat16)
    local = (up * (mix + 1.0)).T

    q_index = lax.broadcasted_iota(jnp.int32, (cuts, 2 * columns, batch), 0)
    for pair in range(pairs):
        weight = jnp.concatenate(
            [
                weight_ref[q * share + pair * 2 * columns : q * share + (pair + 1) * 2 * columns, :]
                for q in range(cuts)
            ],
            axis=0,
        )
        back = dot_nt(weight, mix_grad).reshape(cuts, 2 * columns, batch)
        term = local[pair * 2 * columns : (pair + 1) * 2 * columns]
        back = back + jnp.where(q_index == own, term[None], 0.0)
        at = pair * batch
        turned_s[:, at : at + batch] = back[:, :columns].reshape(lanes, batch).astype(jnp.bfloat16)
        turned_s[:, half + at : half + at + batch] = back[:, columns:].reshape(lanes, batch).astype(jnp.bfloat16)
    slot_grad = dot(turned_s[...], count_ref[...]).T
    parts = swap_blocks([slot_grad[j * owners : (j + 1) * owners] for j in range(cap)], columns)
    for q in range(cuts):
        grad_ref[q] = parts[q].astype(jnp.bfloat16)


def call(kernel, out_shape, in_spaces, scratch=(), limit=48, out_space=pltpu.VMEM, **kw):
    outs = jax.tree.map(lambda unused: pl.BlockSpec(memory_space=out_space), out_shape)
    return pl.pallas_call(
        kernel,
        out_shape=out_shape,
        in_specs=[pl.BlockSpec(memory_space=space) for space in in_spaces],
        out_specs=outs,
        scratch_shapes=list(scratch),
        compiler_params=pltpu.CompilerParams(vmem_limit_bytes=limit * 2**20),
        **kw,
    )


def pick(ids, emb, shards, lanes, **kw):
    scratch = [
        pltpu.VMEM(ids.shape, ids.dtype),
        pltpu.VMEM(emb.shape, emb.dtype),
        pltpu.SemaphoreType.DMA,
        pltpu.SemaphoreType.DMA,
    ]
    out = jax.ShapeDtypeStruct((shards, lanes), jnp.bfloat16)
    return call(pick_kernel, out, [pltpu.HBM, pltpu.HBM], scratch, limit=62, **kw)(ids, emb)


def scatter(ids, grads, rows_out, **kw):
    V = pltpu.VMEM
    return call(scatter_kernel, jax.ShapeDtypeStruct((rows_out, LANES), jnp.float32), [V, V], limit=16, **kw)(ids, grads)


def count(slot, bag, cap, tables, bags, slots, side, **kw):
    V, S = pltpu.VMEM, pltpu.SMEM
    pitch = tables + 1
    rows = (bags // tables - 1) * pitch + tables + window_rows(tables, pitch)
    rows = (rows + 7) // 8 * 8
    width = slots // 2
    out = jax.ShapeDtypeStruct((bags, width), jnp.bfloat16)
    return call(
        functools.partial(count_kernel, cap, slots // cap, tables, pitch, side * width),
        out,
        [S, V, V],
        [
            pltpu.VMEM((width // LANES, rows, LANES), jnp.float32),
            pltpu.VMEM(out.shape, out.dtype),
            pltpu.SemaphoreType.DMA((8,)),
        ],
        out_space=pltpu.HBM,
        limit=58,
        **kw,
    )(bag, slot, bag)


def cross(own, rows, low, high, weight, bias, up, cap, **kw):
    V, S, H = pltpu.VMEM, pltpu.SMEM, pltpu.HBM
    cuts, owners, lanes = rows.shape
    batch, share = up.shape
    bags = low.shape[0]
    return call(
        functools.partial(cross_kernel, cap),
        (jax.ShapeDtypeStruct(up.shape, jnp.bfloat16), jax.ShapeDtypeStruct(rows.shape, jnp.bfloat16)),
        [S, V, H, H, V, V, V],
        [
            pltpu.VMEM((bags, 2 * low.shape[1]), jnp.bfloat16),
            pltpu.VMEM((bags // 2, 2 * lanes), jnp.bfloat16),
            pltpu.VMEM((lanes, bags), jnp.bfloat16),
            pltpu.SemaphoreType.DMA((bags // (2 * batch),)),
        ],
        limit=48,
        **kw,
    )(own, rows, low, high, weight, bias, up)


def per_device(embedding, cross_weight, cross_bias, upstream, unique_rows, lookup_slot, bag_of_lookup):
    owners = lax.axis_size("table")
    cuts = lax.axis_size("cuts")
    rows_dev, columns = embedding.shape
    cap = unique_rows.shape[2]
    batch, share = upstream.shape
    tables = share // columns
    lanes = cap * columns
    highs = rows_dev // LANES
    ids = unique_rows[:, 0, :].T
    emb = embedding.T.reshape(columns, highs, LANES).transpose(1, 0, 2).reshape(highs * columns, LANES)
    picked = pick(ids, emb, owners, lanes)
    arrived = lax.all_to_all(picked, "table", 0, 0, tiled=True)
    sizes = (cap, tables, batch * tables, owners * cap)
    low = count(lookup_slot, bag_of_lookup, *sizes, 0)
    arrived, low, lookup_slot, bag_of_lookup = lax.optimization_barrier(
        (arrived, low, lookup_slot, bag_of_lookup)
    )
    rows = lax.all_to_all(
        jnp.broadcast_to(arrived[None], (cuts,) + arrived.shape), "cuts", 0, 0, tiled=True
    )
    high = count(lookup_slot, bag_of_lookup, *sizes, 1)
    own = lax.axis_index("cuts").astype(jnp.int32).reshape(1)
    cross_out, grads = cross(own, rows, low, high, cross_weight, cross_bias.reshape(1, share), upstream, cap)
    grads = lax.all_to_all(grads, "cuts", 0, 0, tiled=True)
    grads = jnp.sum(grads.astype(jnp.float32), axis=0).astype(jnp.bfloat16)
    returned = lax.all_to_all(grads, "table", 0, 0, tiled=True)
    row_grads = scatter(ids, returned, highs * columns)
    row_grads = row_grads.reshape(highs, columns, LANES).transpose(1, 0, 2).reshape(columns, rows_dev).T
    return cross_out, row_grads


def solution(mesh):
    return jax.shard_map(
        per_device,
        mesh=mesh,
        in_specs=(
            P("table", "cuts"),
            P(None, "cuts"),
            P("cuts"),
            P("table", "cuts"),
            P(None, "table", None),
            P("table", None),
            P("table", None),
        ),
        out_specs=(P("table", "cuts"), P("table", "cuts")),
        check_vma=False,
    )
```

```python
import functools

import jax
import jax.numpy as jnp
from jax import lax
from jax.experimental import pallas as pl
from jax.experimental.pallas import tpu as pltpu
from jax.sharding import PartitionSpec as P

LANES = 128
LOOK_BLOCK = 256
UNROLL = 8
NT = (((1,), (1,)), ((), ()))


def dot(a, b):
    return jnp.dot(a, b, preferred_element_type=jnp.float32)


def dot_nt(a, b):
    return lax.dot_general(a, b, NT, preferred_element_type=jnp.float32)


def one_hot(hit):
    return hit.astype(jnp.float32).astype(jnp.bfloat16)


def window_rows(tables, pitch):
    return (LOOK_BLOCK + 8 + (LOOK_BLOCK // tables + 1) * (pitch - tables) + 7) // 8 * 8


def swap_blocks(parts, width):
    parts = list(parts)
    count = len(parts)
    lanes = parts[0].shape[1]
    block = lax.broadcasted_iota(jnp.int32, parts[0].shape, 1) // width
    step = 1
    while step < count:
        high = (block & step) != 0
        for a in range(count):
            if a & step:
                continue
            low_part, high_part = parts[a], parts[a | step]
            parts[a] = jnp.where(high, pltpu.roll(high_part, step * width, 1), low_part)
            parts[a | step] = jnp.where(
                high, high_part, pltpu.roll(low_part, lanes - step * width, 1)
            )
        step *= 2
    return parts


def row_halves(ids_ref, group, per):
    ids = jnp.concatenate([ids_ref[group * per + k : group * per + k + 1, :] for k in range(per)], axis=1)
    return ids // LANES, ids % LANES


def pick_kernel(ids_hbm, emb_hbm, out_ref, ids_ref, emb_ref, ids_sem, emb_sem):
    emb_copy = pltpu.make_async_copy(emb_hbm, emb_ref, emb_sem)
    ids_copy = pltpu.make_async_copy(ids_hbm, ids_ref, ids_sem)
    emb_copy.start()
    ids_copy.start()
    ids_copy.wait()
    emb_copy.wait()
    cap, shards = ids_ref.shape
    columns = out_ref.shape[2] // cap
    highs = emb_ref.shape[0] // columns
    per = 256 // shards
    pieces = []
    for group in range(cap // per):
        hi, lo = row_halves(ids_ref, group, per)
        n = hi.shape[1]
        low_hot = one_hot(lax.broadcasted_iota(jnp.int32, (LANES, n), 0) == lo)
        wide = dot(emb_ref[...], low_hot).reshape(highs, columns, n)
        high_hot = lax.broadcasted_iota(jnp.int32, (highs, columns, n), 0) == hi[None]
        found = jnp.sum(jnp.where(high_hot, wide, 0.0), axis=0)
        for k in range(per):
            pieces.append(found[:, k * shards : (k + 1) * shards])
    out_ref[:, 0, :] = jnp.concatenate(pieces, axis=0).T.astype(out_ref.dtype)


def scatter_kernel(ids_ref, grad_ref, out_ref):
    cap, shards = ids_ref.shape
    columns = grad_ref.shape[1] // cap
    highs = out_ref.shape[0] // columns
    per = 256 // shards
    turned = grad_ref[...].astype(jnp.float32).T
    for group in range(cap // per):
        hi, lo = row_halves(ids_ref, group, per)
        n = hi.shape[1]
        low_hot = one_hot(lax.broadcasted_iota(jnp.int32, (LANES, n), 0) == lo)
        values = jnp.concatenate(
            [turned[(group * per + k) * columns : (group * per + k + 1) * columns] for k in range(per)],
            axis=1,
        )
        high_hot = lax.broadcasted_iota(jnp.int32, (highs, columns, n), 0) == hi[None]
        spread = jnp.where(high_hot, values[None], 0.0).reshape(highs * columns, n).astype(jnp.bfloat16)
        part = dot_nt(spread, low_hot)
        if group == 0:
            out_ref[...] = part
        else:
            out_ref[...] += part


def low_kernel(cap, owners, tables, pitch, firsts_ref, slot_ref, bag_ref, out_hbm, acc, out_ref, sems):
    rows = out_ref.shape[0] // sems.shape[0]
    copies = []
    for c in range(sems.shape[0]):
        done = pl.ds(c * rows, rows)
        copies.append(pltpu.make_async_copy(out_ref.at[done], out_hbm.at[done], sems.at[c]))

    def flush(row):
        if row % rows == 0:
            copies[row // rows - 1].start()

    count_slots(cap, owners, tables, pitch, 0, firsts_ref, slot_ref, bag_ref, out_ref, acc, flush)
    for copy in copies:
        copy.wait()


def count_slots(cap, owners, tables, pitch, first_slot, firsts_ref, slot_ref, bag_ref, out_ref, acc, flush):
    look = slot_ref.shape[1]
    slots = out_ref.shape[1]
    batch = out_ref.shape[0] // tables
    gap = pitch - tables
    window = window_rows(tables, pitch)
    for n in range(slots // LANES):
        acc[n, 0:8, :] = jnp.zeros((8, LANES), jnp.float32)

    def body(i, carry):
        at = pl.ds(pl.multiple_of(i * LOOK_BLOCK, LOOK_BLOCK), LOOK_BLOCK)
        first = firsts_ref[0, i * LOOK_BLOCK]
        start = pl.multiple_of((first + first // tables * gap) // 8 * 8, 8)
        bags = bag_ref[:, at]
        bags = bags + bags // tables * gap - start
        slot = slot_ref[:, at]
        order = slot % cap * owners + slot // cap - first_slot
        bag_hot = one_hot(lax.broadcasted_iota(jnp.int32, (window, LOOK_BLOCK), 0) == bags)
        for n in range(slots // 256):
            slot_hot = one_hot(lax.broadcasted_iota(jnp.int32, (256, LOOK_BLOCK), 0) + n * 256 == order)
            part = dot_nt(bag_hot, slot_hot)
            for m in range(2):
                cols = slice(m * LANES, (m + 1) * LANES)
                acc[2 * n + m, pl.ds(start, 8), :] += part[0:8, cols]
                acc[2 * n + m, pl.ds(start + 8, window - 8), :] = part[8:, cols]
        return carry

    lax.fori_loop(0, look // LOOK_BLOCK, body, 0, unroll=UNROLL)
    half = tables // 2
    for place in range(tables):
        f = place % half * 2 + place // half
        row = place * batch
        for n in range(slots // LANES):
            cols = slice(n * LANES, (n + 1) * LANES)
            out_ref[row : row + batch, cols] = acc[n, pl.ds(f, batch, stride=pitch), :].astype(jnp.bfloat16)
        flush(row + batch)


def cross_kernel(
    cap, tables, pitch, own_ref, firsts_ref, slot_ref, bag_ref, low_hbm, rows_ref, weight_ref, bias_ref, up_ref,
    out_ref, grad_ref, count_ref, acc, base_s, turned_s, low_sem,
):
    cuts, owners, lanes = rows_ref.shape
    columns = lanes // cap
    batch, share = up_ref.shape
    pairs = share // (2 * columns)
    own = own_ref[0]
    half = pairs * batch
    chunk = 4 * batch

    width = low_hbm.shape[1]
    low_copy = pltpu.make_async_copy(low_hbm, count_ref.at[:, pl.ds(0, width)], low_sem)
    low_copy.start()
    high = count_ref.at[:, pl.ds(width, width)]
    count_slots(
        cap, owners, tables, pitch, width, firsts_ref, slot_ref, bag_ref, high, acc, lambda row: None
    )

    picked = swap_blocks([rows_ref[q].astype(jnp.float32) for q in range(cuts)], columns)
    rows = jnp.concatenate(picked, axis=0).astype(jnp.bfloat16)
    wide = 2 * lanes
    r = lax.broadcasted_iota(jnp.int32, (lanes, wide), 0)
    l = lax.broadcasted_iota(jnp.int32, (lanes, wide), 1)
    same = (l // (2 * columns) == r // columns) & (l % columns == r % columns)
    odd = (l // columns) % 2 == 1
    put_even = jnp.where(same & ~odd, 1.0, 0.0).astype(jnp.bfloat16)
    put_odd = jnp.where(same & odd, 1.0, 0.0).astype(jnp.bfloat16)
    rows_even = dot(rows, put_even).astype(jnp.bfloat16)
    rows_odd = dot(rows, put_odd).astype(jnp.bfloat16)

    low_copy.wait()
    for c in range(half // chunk):
        at = c * chunk
        both = dot(count_ref[at : at + chunk, :], rows_even) + dot(
            count_ref[half + at : half + at + chunk, :], rows_odd
        )
        base_s[at : at + chunk, :] = both.astype(jnp.bfloat16)

    lane_block = lax.broadcasted_iota(jnp.int32, (batch, lanes), 1) // (2 * columns)
    per_half = lanes // (2 * columns)
    mix = jnp.zeros((batch, share), jnp.float32)
    own_base = [jnp.zeros((batch, lanes), jnp.float32) for _ in range(2)]
    weights = []
    for pair in range(pairs):
        base = base_s[pair * batch : (pair + 1) * batch, :]
        weight = jnp.concatenate(
            [
                weight_ref[q * share + pair * 2 * columns : q * share + (pair + 1) * 2 * columns, :]
                for q in range(cuts)
            ],
            axis=0,
        )
        mix = mix + dot(base, weight)
        mine = jnp.where(own < cuts // 2, base[:, :lanes].astype(jnp.float32), base[:, lanes:].astype(jnp.float32))
        shift = (pair % per_half - own % per_half + per_half) % per_half * (2 * columns)
        moved = pltpu.roll(mine, shift, 1)
        side = pair // per_half
        own_base[side] = jnp.where(lane_block == pair % per_half, moved, own_base[side])
    base_wide = jnp.concatenate(own_base, axis=1)
    mix = mix + bias_ref[...]
    out_ref[...] = (base_wide * mix + base_wide).astype(jnp.bfloat16)
    up = up_ref[...].astype(jnp.float32)
    mix_grad = (up * base_wide).astype(jnp.bfloat16)
    local = (up * (mix + 1.0)).T

    q_index = lax.broadcasted_iota(jnp.int32, (cuts, 2 * columns, batch), 0)
    for pair in range(pairs):
        weight = jnp.concatenate(
            [
                weight_ref[q * share + pair * 2 * columns : q * share + (pair + 1) * 2 * columns, :]
                for q in range(cuts)
            ],
            axis=0,
        )
        back = dot_nt(weight, mix_grad).reshape(cuts, 2 * columns, batch)
        term = local[pair * 2 * columns : (pair + 1) * 2 * columns]
        back = back + jnp.where(q_index == own, term[None], 0.0)
        at = pair * batch
        turned_s[:, at : at + batch] = back[:, :columns].reshape(lanes, batch).astype(jnp.bfloat16)
        turned_s[:, half + at : half + at + batch] = back[:, columns:].reshape(lanes, batch).astype(jnp.bfloat16)
    slot_grad = dot(turned_s[...], count_ref[...]).T
    parts = swap_blocks([slot_grad[j * owners : (j + 1) * owners] for j in range(cap)], columns)
    for q in range(cuts):
        grad_ref[q] = parts[q].astype(jnp.bfloat16)


def call(kernel, out_shape, in_spaces, scratch=(), limit=48, out_space=pltpu.VMEM, **kw):
    outs = jax.tree.map(lambda unused: pl.BlockSpec(memory_space=out_space), out_shape)
    return pl.pallas_call(
        kernel,
        out_shape=out_shape,
        in_specs=[pl.BlockSpec(memory_space=space) for space in in_spaces],
        out_specs=outs,
        scratch_shapes=list(scratch),
        compiler_params=pltpu.CompilerParams(vmem_limit_bytes=limit * 2**20),
        **kw,
    )


def pick(ids, emb, shards, lanes, **kw):
    scratch = [
        pltpu.VMEM(ids.shape, ids.dtype),
        pltpu.VMEM(emb.shape, emb.dtype),
        pltpu.SemaphoreType.DMA,
        pltpu.SemaphoreType.DMA,
    ]
    out = jax.ShapeDtypeStruct((shards, 1, lanes), jnp.bfloat16)
    return call(pick_kernel, out, [pltpu.HBM, pltpu.HBM], scratch, limit=62, **kw)(ids, emb)


def scatter(ids, grads, rows_out, **kw):
    V = pltpu.VMEM
    return call(scatter_kernel, jax.ShapeDtypeStruct((rows_out, LANES), jnp.float32), [V, V], limit=16, **kw)(ids, grads)


def count_scratch(slots, bags, tables):
    pitch = tables + 1
    rows = (bags // tables - 1) * pitch + tables + window_rows(tables, pitch)
    rows = (rows + 7) // 8 * 8
    return pitch, pltpu.VMEM((slots // LANES, rows, LANES), jnp.float32)


def count_low(slot, bag, cap, tables, bags, slots, **kw):
    V, S = pltpu.VMEM, pltpu.SMEM
    out = jax.ShapeDtypeStruct((bags, slots // 2), jnp.bfloat16)
    pitch, acc = count_scratch(slots // 2, bags, tables)
    return call(
        functools.partial(low_kernel, cap, slots // cap, tables, pitch),
        out,
        [S, V, V],
        [acc, pltpu.VMEM(out.shape, out.dtype), pltpu.SemaphoreType.DMA((8,))],
        out_space=pltpu.HBM,
        limit=58,
        **kw,
    )(bag, slot, bag)


def cross(own, slot, bag, low, rows, weight, bias, up, cap, **kw):
    V, S = pltpu.VMEM, pltpu.SMEM
    cuts, owners, lanes = rows.shape
    bags, width = low.shape
    tables = bags // up.shape[0]
    pitch, acc = count_scratch(width, bags, tables)
    return call(
        functools.partial(cross_kernel, cap, tables, pitch),
        (jax.ShapeDtypeStruct(up.shape, jnp.bfloat16), jax.ShapeDtypeStruct(rows.shape, jnp.bfloat16)),
        [S, S, V, V, pltpu.HBM, V, V, V, V],
        [
            pltpu.VMEM((bags, 2 * width), jnp.bfloat16),
            acc,
            pltpu.VMEM((bags // 2, 2 * lanes), jnp.bfloat16),
            pltpu.VMEM((lanes, bags), jnp.bfloat16),
            pltpu.SemaphoreType.DMA,
        ],
        limit=48,
        **kw,
    )(own, bag, slot, bag, low, rows, weight, bias, up)


def per_device(embedding, cross_weight, cross_bias, upstream, unique_rows, lookup_slot, bag_of_lookup):
    owners = lax.axis_size("table")
    cuts = lax.axis_size("cuts")
    rows_dev, columns = embedding.shape
    cap = unique_rows.shape[2]
    batch, share = upstream.shape
    tables = share // columns
    lanes = cap * columns
    highs = rows_dev // LANES
    ids = unique_rows[:, 0, :].T
    emb = embedding.T.reshape(columns, highs, LANES).transpose(1, 0, 2).reshape(highs * columns, LANES)
    picked = pick(ids, emb, owners, lanes)
    arrived = lax.all_to_all(picked, "table", 0, 0, tiled=True)
    sizes = (cap, tables, batch * tables, owners * cap)
    low = count_low(lookup_slot, bag_of_lookup, *sizes)
    arrived, low = lax.optimization_barrier((arrived, low))
    rows = lax.all_to_all(
        jnp.broadcast_to(arrived.reshape(1, owners, lanes), (cuts, owners, lanes)), "cuts", 0, 0, tiled=True
    )
    own = lax.axis_index("cuts").astype(jnp.int32).reshape(1)
    cross_out, grads = cross(
        own, lookup_slot, bag_of_lookup, low, rows, cross_weight, cross_bias.reshape(1, share), upstream, cap
    )
    grads = lax.all_to_all(grads, "cuts", 0, 0, tiled=True)
    grads = jnp.sum(grads.astype(jnp.float32), axis=0).astype(jnp.bfloat16)
    returned = lax.all_to_all(grads, "table", 0, 0, tiled=True)
    row_grads = scatter(ids, returned, highs * columns)
    row_grads = row_grads.reshape(highs, columns, LANES).transpose(1, 0, 2).reshape(columns, rows_dev).T
    return cross_out, row_grads


def solution(mesh):
    return jax.shard_map(
        per_device,
        mesh=mesh,
        in_specs=(
            P("table", "cuts"),
            P(None, "cuts"),
            P("cuts"),
            P("table", "cuts"),
            P(None, "table", None),
            P("table", None),
            P("table", None),
        ),
        out_specs=(P("table", "cuts"), P("table", "cuts")),
        check_vma=False,
    )
```

```python
import functools

import jax
import jax.numpy as jnp
from jax import lax
from jax.experimental import pallas as pl
from jax.experimental.pallas import tpu as pltpu
from jax.sharding import PartitionSpec as P

LANES = 128
LOOK_BLOCK = 256
UNROLL = 8
NT = (((1,), (1,)), ((), ()))


def dot(a, b):
    return jnp.dot(a, b, preferred_element_type=jnp.float32)


def dot_nt(a, b):
    return lax.dot_general(a, b, NT, preferred_element_type=jnp.float32)


def one_hot(hit):
    return hit.astype(jnp.float32).astype(jnp.bfloat16)


def window_rows(tables, pitch):
    return (LOOK_BLOCK + 8 + (LOOK_BLOCK // tables + 1) * (pitch - tables) + 7) // 8 * 8


def swap_blocks(parts, width):
    parts = list(parts)
    count = len(parts)
    lanes = parts[0].shape[1]
    block = lax.broadcasted_iota(jnp.int32, parts[0].shape, 1) // width
    step = 1
    while step < count:
        high = (block & step) != 0
        for a in range(count):
            if a & step:
                continue
            low_part, high_part = parts[a], parts[a | step]
            parts[a] = jnp.where(high, pltpu.roll(high_part, step * width, 1), low_part)
            parts[a | step] = jnp.where(
                high, high_part, pltpu.roll(low_part, lanes - step * width, 1)
            )
        step *= 2
    return parts


def row_halves(ids_ref, group, per):
    ids = jnp.concatenate([ids_ref[group * per + k : group * per + k + 1, :] for k in range(per)], axis=1)
    return ids // LANES, ids % LANES


def pick_kernel(ids_hbm, emb_hbm, out_ref, ids_ref, emb_ref, ids_sem, emb_sem):
    emb_copy = pltpu.make_async_copy(emb_hbm, emb_ref, emb_sem)
    ids_copy = pltpu.make_async_copy(ids_hbm, ids_ref, ids_sem)
    emb_copy.start()
    ids_copy.start()
    ids_copy.wait()
    emb_copy.wait()
    cap, shards = ids_ref.shape
    columns = out_ref.shape[2] // cap
    highs = emb_ref.shape[0] // columns
    per = 256 // shards
    pieces = []
    for group in range(cap // per):
        hi, lo = row_halves(ids_ref, group, per)
        n = hi.shape[1]
        low_hot = one_hot(lax.broadcasted_iota(jnp.int32, (LANES, n), 0) == lo)
        wide = dot(emb_ref[...], low_hot).reshape(highs, columns, n)
        high_hot = lax.broadcasted_iota(jnp.int32, (highs, columns, n), 0) == hi[None]
        found = jnp.sum(jnp.where(high_hot, wide, 0.0), axis=0)
        for k in range(per):
            pieces.append(found[:, k * shards : (k + 1) * shards])
    out_ref[:, 0, :] = jnp.concatenate(pieces, axis=0).T.astype(out_ref.dtype)


def scatter_kernel(ids_ref, grad_ref, out_ref):
    cap, shards = ids_ref.shape
    columns = grad_ref.shape[1] // cap
    highs = out_ref.shape[0] // columns
    per = 256 // shards
    turned = grad_ref[...].astype(jnp.float32).T
    for group in range(cap // per):
        hi, lo = row_halves(ids_ref, group, per)
        n = hi.shape[1]
        low_hot = one_hot(lax.broadcasted_iota(jnp.int32, (LANES, n), 0) == lo)
        values = jnp.concatenate(
            [turned[(group * per + k) * columns : (group * per + k + 1) * columns] for k in range(per)],
            axis=1,
        )
        high_hot = lax.broadcasted_iota(jnp.int32, (highs, columns, n), 0) == hi[None]
        spread = jnp.where(high_hot, values[None], 0.0).reshape(highs * columns, n).astype(jnp.bfloat16)
        part = dot_nt(spread, low_hot)
        if group == 0:
            out_ref[...] = part
        else:
            out_ref[...] += part


def count_kernel(cap, tables, pitch, firsts_ref, slot_ref, bag_ref, out_hbm, acc, out_ref, sems):
    look = slot_ref.shape[1]
    slots = out_ref.shape[1]
    owners = slots // cap
    batch = out_ref.shape[0] // tables
    gap = pitch - tables
    window = window_rows(tables, pitch)
    for n in range(slots // LANES):
        acc[n, 0:8, :] = jnp.zeros((8, LANES), jnp.float32)

    def body(i, carry):
        at = pl.ds(pl.multiple_of(i * LOOK_BLOCK, LOOK_BLOCK), LOOK_BLOCK)
        first = firsts_ref[0, i * LOOK_BLOCK]
        start = pl.multiple_of((first + first // tables * gap) // 8 * 8, 8)
        bags = bag_ref[:, at]
        bags = bags + bags // tables * gap - start
        slot = slot_ref[:, at]
        order = slot % cap * owners + slot // cap
        bag_hot = one_hot(lax.broadcasted_iota(jnp.int32, (window, LOOK_BLOCK), 0) == bags)
        for n in range(slots // 256):
            slot_hot = one_hot(lax.broadcasted_iota(jnp.int32, (256, LOOK_BLOCK), 0) + n * 256 == order)
            part = dot_nt(bag_hot, slot_hot)
            for m in range(2):
                cols = slice(m * LANES, (m + 1) * LANES)
                acc[2 * n + m, pl.ds(start, 8), :] += part[0:8, cols]
                acc[2 * n + m, pl.ds(start + 8, window - 8), :] = part[8:, cols]
        return carry

    lax.fori_loop(0, look // LOOK_BLOCK, body, 0, unroll=UNROLL)
    half = tables // 2
    chunk = tables // sems.shape[0] * batch
    copies = []
    for place in range(tables):
        f = place % half * 2 + place // half
        row = place * batch
        for n in range(slots // LANES):
            cols = slice(n * LANES, (n + 1) * LANES)
            counts = acc[n, pl.ds(f, batch, stride=pitch), :]
            out_ref[row : row + batch, cols] = counts.astype(out_ref.dtype)
        if (row + batch) % chunk == 0:
            done = pl.ds(row + batch - chunk, chunk)
            copies.append(pltpu.make_async_copy(out_ref.at[done], out_hbm.at[done], sems.at[len(copies)]))
            copies[-1].start()
    for copy in copies:
        copy.wait()


def cross_kernel(
    cap, own_ref, count_hbm, rows_ref, weight_ref, bias_ref, up_ref, out_ref, grad_ref,
    small_ref, count_ref, base_s, turned_s, sems,
):
    cuts, owners, lanes = rows_ref.shape
    columns = lanes // cap
    batch, share = up_ref.shape
    pairs = share // (2 * columns)
    own = own_ref[0]
    half = pairs * batch
    chunk = 4 * batch
    copies = []
    for c in range(half // chunk):
        for side in range(2):
            part = pl.ds(side * half + c * chunk, chunk)
            copies.append(pltpu.make_async_copy(count_hbm.at[part], small_ref.at[part], sems.at[2 * c + side]))
            copies[-1].start()

    picked = swap_blocks([rows_ref[q].astype(jnp.float32) for q in range(cuts)], columns)
    rows = jnp.concatenate(picked, axis=0).astype(jnp.bfloat16)
    wide = 2 * lanes
    r = lax.broadcasted_iota(jnp.int32, (lanes, wide), 0)
    l = lax.broadcasted_iota(jnp.int32, (lanes, wide), 1)
    same = (l // (2 * columns) == r // columns) & (l % columns == r % columns)
    odd = (l // columns) % 2 == 1
    put_even = jnp.where(same & ~odd, 1.0, 0.0).astype(jnp.bfloat16)
    put_odd = jnp.where(same & odd, 1.0, 0.0).astype(jnp.bfloat16)
    rows_even = dot(rows, put_even).astype(jnp.bfloat16)
    rows_odd = dot(rows, put_odd).astype(jnp.bfloat16)

    for copy in copies:
        copy.wait()
    for c in range(half // chunk):
        at = c * chunk
        for side in range(2):
            part = slice(side * half + at, side * half + at + chunk)
            count_ref[part, :] = small_ref[part, :].astype(jnp.bfloat16)
        both = dot(count_ref[at : at + chunk, :], rows_even) + dot(
            count_ref[half + at : half + at + chunk, :], rows_odd
        )
        base_s[at : at + chunk, :] = both.astype(jnp.bfloat16)

    lane_block = lax.broadcasted_iota(jnp.int32, (batch, lanes), 1) // (2 * columns)
    per_half = lanes // (2 * columns)
    mix = jnp.zeros((batch, share), jnp.float32)
    own_base = [jnp.zeros((batch, lanes), jnp.float32) for _ in range(2)]
    weights = []
    for pair in range(pairs):
        base = base_s[pair * batch : (pair + 1) * batch, :]
        weight = jnp.concatenate(
            [
                weight_ref[q * share + pair * 2 * columns : q * share + (pair + 1) * 2 * columns, :]
                for q in range(cuts)
            ],
            axis=0,
        )
        mix = mix + dot(base, weight)
        mine = jnp.where(own < cuts // 2, base[:, :lanes].astype(jnp.float32), base[:, lanes:].astype(jnp.float32))
        shift = (pair % per_half - own % per_half + per_half) % per_half * (2 * columns)
        moved = pltpu.roll(mine, shift, 1)
        side = pair // per_half
        own_base[side] = jnp.where(lane_block == pair % per_half, moved, own_base[side])
    base_wide = jnp.concatenate(own_base, axis=1)
    mix = mix + bias_ref[...]
    out_ref[...] = (base_wide * mix + base_wide).astype(jnp.bfloat16)
    up = up_ref[...].astype(jnp.float32)
    mix_grad = (up * base_wide).astype(jnp.bfloat16)
    local = (up * (mix + 1.0)).T

    q_index = lax.broadcasted_iota(jnp.int32, (cuts, 2 * columns, batch), 0)
    for pair in range(pairs):
        weight = jnp.concatenate(
            [
                weight_ref[q * share + pair * 2 * columns : q * share + (pair + 1) * 2 * columns, :]
                for q in range(cuts)
            ],
            axis=0,
        )
        back = dot_nt(weight, mix_grad).reshape(cuts, 2 * columns, batch)
        term = local[pair * 2 * columns : (pair + 1) * 2 * columns]
        back = back + jnp.where(q_index == own, term[None], 0.0)
        at = pair * batch
        turned_s[:, at : at + batch] = back[:, :columns].reshape(lanes, batch).astype(jnp.bfloat16)
        turned_s[:, half + at : half + at + batch] = back[:, columns:].reshape(lanes, batch).astype(jnp.bfloat16)
    slot_grad = dot(turned_s[...], count_ref[...]).T
    parts = swap_blocks([slot_grad[j * owners : (j + 1) * owners] for j in range(cap)], columns)
    for q in range(cuts):
        grad_ref[q] = parts[q].astype(jnp.bfloat16)


def call(kernel, out_shape, in_spaces, scratch=(), limit=48, out_space=pltpu.VMEM, **kw):
    outs = jax.tree.map(lambda unused: pl.BlockSpec(memory_space=out_space), out_shape)
    return pl.pallas_call(
        kernel,
        out_shape=out_shape,
        in_specs=[pl.BlockSpec(memory_space=space) for space in in_spaces],
        out_specs=outs,
        scratch_shapes=list(scratch),
        compiler_params=pltpu.CompilerParams(vmem_limit_bytes=limit * 2**20),
        **kw,
    )


def pick(ids, emb, shards, lanes, **kw):
    scratch = [
        pltpu.VMEM(ids.shape, ids.dtype),
        pltpu.VMEM(emb.shape, emb.dtype),
        pltpu.SemaphoreType.DMA,
        pltpu.SemaphoreType.DMA,
    ]
    out = jax.ShapeDtypeStruct((shards, 1, lanes), jnp.bfloat16)
    return call(pick_kernel, out, [pltpu.HBM, pltpu.HBM], scratch, limit=62, **kw)(ids, emb)


def scatter(ids, grads, rows_out, **kw):
    V = pltpu.VMEM
    return call(scatter_kernel, jax.ShapeDtypeStruct((rows_out, LANES), jnp.float32), [V, V], limit=16, **kw)(ids, grads)


def count(slot, bag, cap, tables, bags, slots, **kw):
    V, S = pltpu.VMEM, pltpu.SMEM
    out = jax.ShapeDtypeStruct((bags, slots), jnp.int8)
    pitch = tables + 1
    rows = (bags // tables - 1) * pitch + tables + window_rows(tables, pitch)
    rows = (rows + 7) // 8 * 8
    return call(
        functools.partial(count_kernel, cap, tables, pitch),
        out,
        [S, V, V],
        [
            pltpu.VMEM((slots // LANES, rows, LANES), jnp.float32),
            pltpu.VMEM(out.shape, out.dtype),
            pltpu.SemaphoreType.DMA((8,)),
        ],
        out_space=pltpu.HBM,
        limit=58,
        **kw,
    )(bag, slot, bag)


def cross(own, counts, rows, weight, bias, up, cap, **kw):
    V, S = pltpu.VMEM, pltpu.SMEM
    cuts, owners, lanes = rows.shape
    bags, slots = counts.shape
    batch = up.shape[0]
    return call(
        functools.partial(cross_kernel, cap),
        (jax.ShapeDtypeStruct(up.shape, jnp.bfloat16), jax.ShapeDtypeStruct(rows.shape, jnp.bfloat16)),
        [S, pltpu.HBM, V, V, V, V],
        [
            pltpu.VMEM(counts.shape, counts.dtype),
            pltpu.VMEM(counts.shape, jnp.bfloat16),
            pltpu.VMEM((bags // 2, 2 * lanes), jnp.bfloat16),
            pltpu.VMEM((lanes, bags), jnp.bfloat16),
            pltpu.SemaphoreType.DMA((bags // (4 * batch),)),
        ],
        limit=48,
        **kw,
    )(own, counts, rows, weight, bias, up)


def per_device(embedding, cross_weight, cross_bias, upstream, unique_rows, lookup_slot, bag_of_lookup):
    owners = lax.axis_size("table")
    cuts = lax.axis_size("cuts")
    rows_dev, columns = embedding.shape
    cap = unique_rows.shape[2]
    batch, share = upstream.shape
    tables = share // columns
    lanes = cap * columns
    highs = rows_dev // LANES
    ids = unique_rows[:, 0, :].T
    emb = embedding.T.reshape(columns, highs, LANES).transpose(1, 0, 2).reshape(highs * columns, LANES)
    picked = pick(ids, emb, owners, lanes)
    arrived = lax.all_to_all(picked, "table", 0, 0, tiled=True)
    sizes = (cap, tables, batch * tables, owners * cap)
    counts = count(lookup_slot, bag_of_lookup, *sizes)
    arrived, counts = lax.optimization_barrier((arrived, counts))
    rows = lax.all_to_all(
        jnp.broadcast_to(arrived.reshape(1, owners, lanes), (cuts, owners, lanes)), "cuts", 0, 0, tiled=True
    )
    own = lax.axis_index("cuts").astype(jnp.int32).reshape(1)
    cross_out, grads = cross(
        own, counts, rows, cross_weight, cross_bias.reshape(1, share), upstream, cap
    )
    grads = lax.all_to_all(grads, "cuts", 0, 0, tiled=True)
    grads = jnp.sum(grads.astype(jnp.float32), axis=0).astype(jnp.bfloat16)
    returned = lax.all_to_all(grads, "table", 0, 0, tiled=True)
    row_grads = scatter(ids, returned, highs * columns)
    row_grads = row_grads.reshape(highs, columns, LANES).transpose(1, 0, 2).reshape(columns, rows_dev).T
    return cross_out, row_grads


def solution(mesh):
    return jax.shard_map(
        per_device,
        mesh=mesh,
        in_specs=(
            P("table", "cuts"),
            P(None, "cuts"),
            P("cuts"),
            P("table", "cuts"),
            P(None, "table", None),
            P("table", None),
            P("table", None),
        ),
        out_specs=(P("table", "cuts"), P("table", "cuts")),
        check_vma=False,
    )
```

```python
import functools

import jax
import jax.numpy as jnp
from jax import lax
from jax.experimental import pallas as pl
from jax.experimental.pallas import tpu as pltpu
from jax.sharding import PartitionSpec as P

LANES = 128
LOOK_BLOCK = 256
UNROLL = 16
NT = (((1,), (1,)), ((), ()))


def dot(a, b):
    return jnp.dot(a, b, preferred_element_type=jnp.float32)


def dot_nt(a, b):
    return lax.dot_general(a, b, NT, preferred_element_type=jnp.float32)


def one_hot(hit):
    return hit.astype(jnp.float32).astype(jnp.bfloat16)


def window_rows(tables, pitch):
    return (LOOK_BLOCK + 8 + (LOOK_BLOCK // tables + 1) * (pitch - tables) + 7) // 8 * 8


def swap_blocks(parts, width):
    parts = list(parts)
    count = len(parts)
    lanes = parts[0].shape[1]
    block = lax.broadcasted_iota(jnp.int32, parts[0].shape, 1) // width
    step = 1
    while step < count:
        high = (block & step) != 0
        for a in range(count):
            if a & step:
                continue
            low_part, high_part = parts[a], parts[a | step]
            parts[a] = jnp.where(high, pltpu.roll(high_part, step * width, 1), low_part)
            parts[a | step] = jnp.where(
                high, high_part, pltpu.roll(low_part, lanes - step * width, 1)
            )
        step *= 2
    return parts


def row_halves(ids_ref, group, per):
    ids = jnp.concatenate([ids_ref[group * per + k : group * per + k + 1, :] for k in range(per)], axis=1)
    return ids // LANES, ids % LANES


def pick_kernel(ids_hbm, emb_hbm, out_ref, ids_ref, emb_ref, ids_sem, emb_sem):
    emb_copy = pltpu.make_async_copy(emb_hbm, emb_ref, emb_sem)
    ids_copy = pltpu.make_async_copy(ids_hbm, ids_ref, ids_sem)
    emb_copy.start()
    ids_copy.start()
    ids_copy.wait()
    emb_copy.wait()
    cap, shards = ids_ref.shape
    columns = out_ref.shape[2] // cap
    highs = emb_ref.shape[0] // columns
    per = 256 // shards
    pieces = []
    for group in range(cap // per):
        hi, lo = row_halves(ids_ref, group, per)
        n = hi.shape[1]
        low_hot = one_hot(lax.broadcasted_iota(jnp.int32, (LANES, n), 0) == lo)
        wide = dot(emb_ref[...], low_hot).reshape(highs, columns, n)
        high_hot = lax.broadcasted_iota(jnp.int32, (highs, columns, n), 0) == hi[None]
        found = jnp.sum(jnp.where(high_hot, wide, 0.0), axis=0)
        for k in range(per):
            pieces.append(found[:, k * shards : (k + 1) * shards])
    out_ref[:, 0, :] = jnp.concatenate(pieces, axis=0).T.astype(out_ref.dtype)


def scatter_kernel(ids_ref, grad_ref, out_ref):
    cap, shards = ids_ref.shape
    columns = grad_ref.shape[1] // cap
    highs = out_ref.shape[0] // columns
    per = 256 // shards
    turned = grad_ref[...].astype(jnp.float32).T
    for group in range(cap // per):
        hi, lo = row_halves(ids_ref, group, per)
        n = hi.shape[1]
        low_hot = one_hot(lax.broadcasted_iota(jnp.int32, (LANES, n), 0) == lo)
        values = jnp.concatenate(
            [turned[(group * per + k) * columns : (group * per + k + 1) * columns] for k in range(per)],
            axis=1,
        )
        high_hot = lax.broadcasted_iota(jnp.int32, (highs, columns, n), 0) == hi[None]
        spread = jnp.where(high_hot, values[None], 0.0).reshape(highs * columns, n).astype(jnp.bfloat16)
        part = dot_nt(spread, low_hot)
        if group == 0:
            out_ref[...] = part
        else:
            out_ref[...] += part


def count_kernel(cap, owners, tables, pitch, first_slot, firsts_ref, slot_ref, bag_ref, out_hbm, acc, out_ref, sems):
    look = slot_ref.shape[1]
    slots = out_ref.shape[1]
    batch = out_ref.shape[0] // tables
    gap = pitch - tables
    window = window_rows(tables, pitch)
    for n in range(slots // LANES):
        acc[n, 0:8, :] = jnp.zeros((8, LANES), jnp.float32)

    def body(i, carry):
        at = pl.ds(pl.multiple_of(i * LOOK_BLOCK, LOOK_BLOCK), LOOK_BLOCK)
        first = firsts_ref[0, i * LOOK_BLOCK]
        start = pl.multiple_of((first + first // tables * gap) // 8 * 8, 8)
        bags = bag_ref[:, at]
        bags = bags + bags // tables * gap - start
        slot = slot_ref[:, at]
        order = slot % cap * owners + slot // cap - first_slot
        bag_hot = one_hot(lax.broadcasted_iota(jnp.int32, (window, LOOK_BLOCK), 0) == bags)
        for n in range(slots // 256):
            slot_hot = one_hot(lax.broadcasted_iota(jnp.int32, (256, LOOK_BLOCK), 0) + n * 256 == order)
            part = dot_nt(bag_hot, slot_hot)
            for m in range(2):
                cols = slice(m * LANES, (m + 1) * LANES)
                acc[2 * n + m, pl.ds(start, 8), :] += part[0:8, cols]
                acc[2 * n + m, pl.ds(start + 8, window - 8), :] = part[8:, cols]
        return carry

    lax.fori_loop(0, look // LOOK_BLOCK, body, 0, unroll=UNROLL)
    half = tables // 2
    chunk = tables // sems.shape[0] * batch
    copies = []
    for place in range(tables):
        f = place % half * 2 + place // half
        row = place * batch
        for n in range(slots // LANES):
            cols = slice(n * LANES, (n + 1) * LANES)
            counts = acc[n, pl.ds(f, batch, stride=pitch), :]
            out_ref[row : row + batch, cols] = counts.astype(out_ref.dtype)
        if (row + batch) % chunk == 0:
            done = pl.ds(row + batch - chunk, chunk)
            copies.append(pltpu.make_async_copy(out_ref.at[done], out_hbm.at[done], sems.at[len(copies)]))
            copies[-1].start()
    for copy in copies:
        copy.wait()


def cross_kernel(
    cap, own_ref, low_hbm, high_hbm, rows_ref, weight_hbm, bias_ref, up_ref, out_ref, grad_ref,
    small_ref, count_ref, weight_ref, base_s, turned_s, sems, weight_sem,
):
    cuts, owners, lanes = rows_ref.shape
    columns = lanes // cap
    batch, share = up_ref.shape
    pairs = share // (2 * columns)
    own = own_ref[0]
    half = pairs * batch
    chunk = 4 * batch
    width = low_hbm.shape[1]
    copies = []
    for k in range(sems.shape[0]):
        source = (low_hbm, high_hbm)[k % 2]
        rows = source.shape[0] * 2 // sems.shape[0]
        part = pl.ds(k // 2 * rows, rows)
        copies.append(pltpu.make_async_copy(source.at[part], small_ref.at[k % 2, part], sems.at[k]))
        copies[-1].start()

    weight_copy = pltpu.make_async_copy(weight_hbm, weight_ref, weight_sem)
    weight_copy.start()

    picked = swap_blocks([rows_ref[q].astype(jnp.float32) for q in range(cuts)], columns)
    rows = jnp.concatenate(picked, axis=0).astype(jnp.bfloat16)
    wide = 2 * lanes
    r = lax.broadcasted_iota(jnp.int32, (lanes, wide), 0)
    l = lax.broadcasted_iota(jnp.int32, (lanes, wide), 1)
    same = (l // (2 * columns) == r // columns) & (l % columns == r % columns)
    odd = (l // columns) % 2 == 1
    put_even = jnp.where(same & ~odd, 1.0, 0.0).astype(jnp.bfloat16)
    put_odd = jnp.where(same & odd, 1.0, 0.0).astype(jnp.bfloat16)
    rows_even = dot(rows, put_even).astype(jnp.bfloat16)
    rows_odd = dot(rows, put_odd).astype(jnp.bfloat16)

    for copy in copies:
        copy.wait()
    weight_copy.wait()
    for c in range(half // chunk):
        at = c * chunk
        for side in range(2):
            part = slice(side * half + at, side * half + at + chunk)
            for k in range(2):
                cols = slice(k * width, (k + 1) * width)
                count_ref[part, cols] = small_ref[k, part, :].astype(jnp.bfloat16)
        both = dot(count_ref[at : at + chunk, :], rows_even) + dot(
            count_ref[half + at : half + at + chunk, :], rows_odd
        )
        base_s[at : at + chunk, :] = both.astype(jnp.bfloat16)

    lane_block = lax.broadcasted_iota(jnp.int32, (batch, lanes), 1) // (2 * columns)
    per_half = lanes // (2 * columns)
    mix = jnp.zeros((batch, share), jnp.float32)
    own_base = [jnp.zeros((batch, lanes), jnp.float32) for _ in range(2)]
    weights = []
    for pair in range(pairs):
        base = base_s[pair * batch : (pair + 1) * batch, :]
        weight = jnp.concatenate(
            [
                weight_ref[q * share + pair * 2 * columns : q * share + (pair + 1) * 2 * columns, :]
                for q in range(cuts)
            ],
            axis=0,
        )
        mix = mix + dot(base, weight)
        mine = jnp.where(own < cuts // 2, base[:, :lanes].astype(jnp.float32), base[:, lanes:].astype(jnp.float32))
        shift = (pair % per_half - own % per_half + per_half) % per_half * (2 * columns)
        moved = pltpu.roll(mine, shift, 1)
        side = pair // per_half
        own_base[side] = jnp.where(lane_block == pair % per_half, moved, own_base[side])
    base_wide = jnp.concatenate(own_base, axis=1)
    mix = mix + bias_ref[...]
    out_ref[...] = (base_wide * mix + base_wide).astype(jnp.bfloat16)
    up = up_ref[...].astype(jnp.float32)
    mix_grad = (up * base_wide).astype(jnp.bfloat16)
    local = (up * (mix + 1.0)).T

    q_index = lax.broadcasted_iota(jnp.int32, (cuts, 2 * columns, batch), 0)
    for pair in range(pairs):
        weight = jnp.concatenate(
            [
                weight_ref[q * share + pair * 2 * columns : q * share + (pair + 1) * 2 * columns, :]
                for q in range(cuts)
            ],
            axis=0,
        )
        back = dot_nt(weight, mix_grad).reshape(cuts, 2 * columns, batch)
        term = local[pair * 2 * columns : (pair + 1) * 2 * columns]
        back = back + jnp.where(q_index == own, term[None], 0.0)
        at = pair * batch
        turned_s[:, at : at + batch] = back[:, :columns].reshape(lanes, batch).astype(jnp.bfloat16)
        turned_s[:, half + at : half + at + batch] = back[:, columns:].reshape(lanes, batch).astype(jnp.bfloat16)
    slot_grad = dot(turned_s[...], count_ref[...]).T
    parts = swap_blocks([slot_grad[j * owners : (j + 1) * owners] for j in range(cap)], columns)
    for q in range(cuts):
        grad_ref[q] = parts[q].astype(jnp.bfloat16)


def call(kernel, out_shape, in_spaces, scratch=(), limit=48, out_space=pltpu.VMEM, **kw):
    outs = jax.tree.map(lambda unused: pl.BlockSpec(memory_space=out_space), out_shape)
    return pl.pallas_call(
        kernel,
        out_shape=out_shape,
        in_specs=[pl.BlockSpec(memory_space=space) for space in in_spaces],
        out_specs=outs,
        scratch_shapes=list(scratch),
        compiler_params=pltpu.CompilerParams(vmem_limit_bytes=limit * 2**20),
        **kw,
    )


def pick(ids, emb, shards, lanes, **kw):
    scratch = [
        pltpu.VMEM(ids.shape, ids.dtype),
        pltpu.VMEM(emb.shape, emb.dtype),
        pltpu.SemaphoreType.DMA,
        pltpu.SemaphoreType.DMA,
    ]
    out = jax.ShapeDtypeStruct((shards, 1, lanes), jnp.bfloat16)
    return call(pick_kernel, out, [pltpu.HBM, pltpu.HBM], scratch, limit=62, **kw)(ids, emb)


def scatter(ids, grads, rows_out, **kw):
    V = pltpu.VMEM
    return call(scatter_kernel, jax.ShapeDtypeStruct((rows_out, LANES), jnp.float32), [V, V], limit=16, **kw)(ids, grads)


def count(slot, bag, cap, tables, bags, slots, side, **kw):
    V, S = pltpu.VMEM, pltpu.SMEM
    width = slots // 2
    out = jax.ShapeDtypeStruct((bags, width), jnp.int8)
    pitch = tables + 1
    rows = (bags // tables - 1) * pitch + tables + window_rows(tables, pitch)
    rows = (rows + 7) // 8 * 8
    return call(
        functools.partial(count_kernel, cap, slots // cap, tables, pitch, side * width),
        out,
        [S, V, V],
        [
            pltpu.VMEM((width // LANES, rows, LANES), jnp.float32),
            pltpu.VMEM(out.shape, out.dtype),
            pltpu.SemaphoreType.DMA((8,)),
        ],
        out_space=pltpu.HBM,
        limit=58,
        **kw,
    )(bag, slot, bag)


def cross(own, low, high, rows, weight, bias, up, cap, **kw):
    V, S = pltpu.VMEM, pltpu.SMEM
    cuts, owners, lanes = rows.shape
    bags, width = low.shape
    return call(
        functools.partial(cross_kernel, cap),
        (jax.ShapeDtypeStruct(up.shape, jnp.bfloat16), jax.ShapeDtypeStruct(rows.shape, jnp.bfloat16)),
        [S, pltpu.HBM, pltpu.HBM, V, pltpu.HBM, V, V],
        [
            pltpu.VMEM((2, bags, width), low.dtype),
            pltpu.VMEM((bags, 2 * width), jnp.bfloat16),
            pltpu.VMEM(weight.shape, weight.dtype),
            pltpu.VMEM((bags // 2, 2 * lanes), jnp.bfloat16),
            pltpu.VMEM((lanes, bags), jnp.bfloat16),
            pltpu.SemaphoreType.DMA((8,)),
            pltpu.SemaphoreType.DMA,
        ],
        limit=50,
        **kw,
    )(own, low, high, rows, weight, bias, up)


def per_device(embedding, cross_weight, cross_bias, upstream, unique_rows, lookup_slot, bag_of_lookup):
    owners = lax.axis_size("table")
    cuts = lax.axis_size("cuts")
    rows_dev, columns = embedding.shape
    cap = unique_rows.shape[2]
    batch, share = upstream.shape
    tables = share // columns
    lanes = cap * columns
    highs = rows_dev // LANES
    ids = unique_rows[:, 0, :].T
    emb = embedding.T.reshape(columns, highs, LANES).transpose(1, 0, 2).reshape(highs * columns, LANES)
    picked = pick(ids, emb, owners, lanes)
    arrived = lax.all_to_all(picked, "table", 0, 0, tiled=True)
    sizes = (cap, tables, batch * tables, owners * cap)
    low = count(lookup_slot, bag_of_lookup, *sizes, 0)
    arrived, low, lookup_slot, bag_of_lookup = lax.optimization_barrier(
        (arrived, low, lookup_slot, bag_of_lookup)
    )
    rows = lax.all_to_all(
        jnp.broadcast_to(arrived.reshape(1, owners, lanes), (cuts, owners, lanes)), "cuts", 0, 0, tiled=True
    )
    high = count(lookup_slot, bag_of_lookup, *sizes, 1)
    own = lax.axis_index("cuts").astype(jnp.int32).reshape(1)
    cross_out, grads = cross(
        own, low, high, rows, cross_weight, cross_bias.reshape(1, share), upstream, cap
    )
    grads = lax.all_to_all(grads, "cuts", 0, 0, tiled=True)
    grads = jnp.sum(grads.astype(jnp.float32), axis=0).astype(jnp.bfloat16)
    returned = lax.all_to_all(grads, "table", 0, 0, tiled=True)
    row_grads = scatter(ids, returned, highs * columns)
    row_grads = row_grads.reshape(highs, columns, LANES).transpose(1, 0, 2).reshape(columns, rows_dev).T
    return cross_out, row_grads


def solution(mesh):
    return jax.shard_map(
        per_device,
        mesh=mesh,
        in_specs=(
            P("table", "cuts"),
            P(None, "cuts"),
            P("cuts"),
            P("table", "cuts"),
            P(None, "table", None),
            P("table", None),
            P("table", None),
        ),
        out_specs=(P("table", "cuts"), P("table", "cuts")),
        check_vma=False,
    )
```

```python
import functools

import jax
import jax.numpy as jnp
from jax import lax
from jax.experimental import pallas as pl
from jax.experimental.pallas import tpu as pltpu
from jax.sharding import PartitionSpec as P

LANES = 128
LOOK_BLOCK = 256
UNROLL = 16
NT = (((1,), (1,)), ((), ()))


def dot(a, b):
    return jnp.dot(a, b, preferred_element_type=jnp.float32)


def dot_nt(a, b):
    return lax.dot_general(a, b, NT, preferred_element_type=jnp.float32)


def one_hot(hit):
    return hit.astype(jnp.float32).astype(jnp.bfloat16)


def window_rows(tables, pitch):
    return (LOOK_BLOCK + 8 + (LOOK_BLOCK // tables + 1) * (pitch - tables) + 7) // 8 * 8


def swap_blocks(parts, width):
    parts = list(parts)
    count = len(parts)
    lanes = parts[0].shape[1]
    block = lax.broadcasted_iota(jnp.int32, parts[0].shape, 1) // width
    step = 1
    while step < count:
        high = (block & step) != 0
        for a in range(count):
            if a & step:
                continue
            low_part, high_part = parts[a], parts[a | step]
            parts[a] = jnp.where(high, pltpu.roll(high_part, step * width, 1), low_part)
            parts[a | step] = jnp.where(
                high, high_part, pltpu.roll(low_part, lanes - step * width, 1)
            )
        step *= 2
    return parts


def row_halves(ids_ref, group, per):
    ids = jnp.concatenate([ids_ref[group * per + k : group * per + k + 1, :] for k in range(per)], axis=1)
    return ids // LANES, ids % LANES


def pick_kernel(ids_hbm, emb_hbm, out_ref, ids_ref, emb_ref, ids_sem, emb_sem):
    emb_copy = pltpu.make_async_copy(emb_hbm, emb_ref, emb_sem)
    ids_copy = pltpu.make_async_copy(ids_hbm, ids_ref, ids_sem)
    emb_copy.start()
    ids_copy.start()
    ids_copy.wait()
    cap, shards = ids_ref.shape
    columns = out_ref.shape[2] // cap
    highs = emb_ref.shape[0] // columns
    per = cap // 2
    pieces = []
    for group in range(cap // per):
        hi, lo = row_halves(ids_ref, group, per)
        n = hi.shape[1]
        low_hot = one_hot(lax.broadcasted_iota(jnp.int32, (LANES, n), 0) == lo)
        if group == 0:
            emb_copy.wait()
        wide = dot(emb_ref[...], low_hot).reshape(highs, columns, n)
        high_hot = lax.broadcasted_iota(jnp.int32, (highs, columns, n), 0) == hi[None]
        found = jnp.sum(jnp.where(high_hot, wide, 0.0), axis=0)
        for k in range(per):
            pieces.append(found[:, k * shards : (k + 1) * shards])
    out_ref[:, 0, :] = jnp.concatenate(pieces, axis=0).T.astype(out_ref.dtype)


def scatter_kernel(ids_ref, grad_ref, out_ref):
    cap, shards = ids_ref.shape
    columns = grad_ref.shape[1] // cap
    highs = out_ref.shape[0] // columns
    per = 256 // shards
    turned = grad_ref[...].astype(jnp.float32).T
    for group in range(cap // per):
        hi, lo = row_halves(ids_ref, group, per)
        n = hi.shape[1]
        low_hot = one_hot(lax.broadcasted_iota(jnp.int32, (LANES, n), 0) == lo)
        values = jnp.concatenate(
            [turned[(group * per + k) * columns : (group * per + k + 1) * columns] for k in range(per)],
            axis=1,
        )
        high_hot = lax.broadcasted_iota(jnp.int32, (highs, columns, n), 0) == hi[None]
        spread = jnp.where(high_hot, values[None], 0.0).reshape(highs * columns, n).astype(jnp.bfloat16)
        part = dot_nt(spread, low_hot)
        if group == 0:
            out_ref[...] = part
        else:
            out_ref[...] += part


def count_kernel(cap, owners, tables, pitch, first_slot, firsts_ref, slot_ref, bag_ref, out_hbm, acc, out_ref, sems):
    look = slot_ref.shape[1]
    slots = out_ref.shape[1]
    batch = out_ref.shape[0] // tables
    gap = pitch - tables
    window = window_rows(tables, pitch)
    for n in range(slots // LANES):
        acc[n, 0:8, :] = jnp.zeros((8, LANES), jnp.float32)

    def body(i, carry):
        at = pl.ds(pl.multiple_of(i * LOOK_BLOCK, LOOK_BLOCK), LOOK_BLOCK)
        first = firsts_ref[0, i * LOOK_BLOCK]
        start = pl.multiple_of((first + first // tables * gap) // 8 * 8, 8)
        bags = bag_ref[:, at]
        bags = bags + bags // tables * gap - start
        slot = slot_ref[:, at]
        order = slot % cap * owners + slot // cap - first_slot
        bag_hot = one_hot(lax.broadcasted_iota(jnp.int32, (window, LOOK_BLOCK), 0) == bags)
        for n in range(slots // 256):
            slot_hot = one_hot(lax.broadcasted_iota(jnp.int32, (256, LOOK_BLOCK), 0) + n * 256 == order)
            part = dot_nt(bag_hot, slot_hot)
            for m in range(2):
                cols = slice(m * LANES, (m + 1) * LANES)
                acc[2 * n + m, pl.ds(start, 8), :] += part[0:8, cols]
                acc[2 * n + m, pl.ds(start + 8, window - 8), :] = part[8:, cols]
        return carry

    lax.fori_loop(0, look // LOOK_BLOCK, body, 0, unroll=UNROLL)
    half = tables // 2
    chunk = tables // sems.shape[0] * batch
    copies = []
    for place in range(tables):
        f = place % half * 2 + place // half
        row = place * batch
        for n in range(slots // LANES):
            cols = slice(n * LANES, (n + 1) * LANES)
            counts = acc[n, pl.ds(f, batch, stride=pitch), :]
            out_ref[row : row + batch, cols] = counts.astype(out_ref.dtype)
        if (row + batch) % chunk == 0:
            done = pl.ds(row + batch - chunk, chunk)
            copies.append(pltpu.make_async_copy(out_ref.at[done], out_hbm.at[done], sems.at[len(copies)]))
            copies[-1].start()
    for copy in copies:
        copy.wait()


def cross_kernel(
    cap, own_ref, low_hbm, high_hbm, rows_ref, weight_hbm, bias_ref, up_ref, out_ref, grad_ref,
    small_ref, count_ref, weight_ref, base_s, turned_s, sems, weight_sem,
):
    cuts, owners, lanes = rows_ref.shape
    columns = lanes // cap
    batch, share = up_ref.shape
    pairs = share // (2 * columns)
    own = own_ref[0]
    half = pairs * batch
    chunk = 4 * batch
    width = low_hbm.shape[1]
    copies = []
    for k in range(sems.shape[0]):
        source = (low_hbm, high_hbm)[k % 2]
        rows = source.shape[0] * 2 // sems.shape[0]
        part = pl.ds(k // 2 * rows, rows)
        copies.append(pltpu.make_async_copy(source.at[part], small_ref.at[k % 2, part], sems.at[k]))
        copies[-1].start()

    weight_copy = pltpu.make_async_copy(weight_hbm, weight_ref, weight_sem)
    weight_copy.start()

    picked = swap_blocks([rows_ref[q].astype(jnp.float32) for q in range(cuts)], columns)
    rows = jnp.concatenate(picked, axis=0).astype(jnp.bfloat16)
    wide = 2 * lanes
    r = lax.broadcasted_iota(jnp.int32, (lanes, wide), 0)
    l = lax.broadcasted_iota(jnp.int32, (lanes, wide), 1)
    same = (l // (2 * columns) == r // columns) & (l % columns == r % columns)
    odd = (l // columns) % 2 == 1
    put_even = jnp.where(same & ~odd, 1.0, 0.0).astype(jnp.bfloat16)
    put_odd = jnp.where(same & odd, 1.0, 0.0).astype(jnp.bfloat16)
    rows_even = dot(rows, put_even).astype(jnp.bfloat16)
    rows_odd = dot(rows, put_odd).astype(jnp.bfloat16)

    for copy in copies:
        copy.wait()
    for c in range(half // chunk):
        at = c * chunk
        for side in range(2):
            part = slice(side * half + at, side * half + at + chunk)
            for k in range(2):
                cols = slice(k * width, (k + 1) * width)
                count_ref[part, cols] = small_ref[k, part, :].astype(jnp.bfloat16)
        both = dot(count_ref[at : at + chunk, :], rows_even) + dot(
            count_ref[half + at : half + at + chunk, :], rows_odd
        )
        base_s[at : at + chunk, :] = both.astype(jnp.bfloat16)

    weight_copy.wait()
    lane_block = lax.broadcasted_iota(jnp.int32, (batch, lanes), 1) // (2 * columns)
    per_half = lanes // (2 * columns)
    mix = jnp.zeros((batch, share), jnp.float32)
    own_base = [jnp.zeros((batch, lanes), jnp.float32) for _ in range(2)]
    weights = []
    for pair in range(pairs):
        base = base_s[pair * batch : (pair + 1) * batch, :]
        weight = jnp.concatenate(
            [
                weight_ref[q * share + pair * 2 * columns : q * share + (pair + 1) * 2 * columns, :]
                for q in range(cuts)
            ],
            axis=0,
        )
        mix = mix + dot(base, weight)
        mine = jnp.where(own < cuts // 2, base[:, :lanes].astype(jnp.float32), base[:, lanes:].astype(jnp.float32))
        shift = (pair % per_half - own % per_half + per_half) % per_half * (2 * columns)
        moved = pltpu.roll(mine, shift, 1)
        side = pair // per_half
        own_base[side] = jnp.where(lane_block == pair % per_half, moved, own_base[side])
    base_wide = jnp.concatenate(own_base, axis=1)
    mix = mix + bias_ref[...]
    out_ref[...] = (base_wide * mix + base_wide).astype(jnp.bfloat16)
    up = up_ref[...].astype(jnp.float32)
    mix_grad = (up * base_wide).astype(jnp.bfloat16)
    local = (up * (mix + 1.0)).T

    q_index = lax.broadcasted_iota(jnp.int32, (cuts, 2 * columns, batch), 0)
    for pair in range(pairs):
        weight = jnp.concatenate(
            [
                weight_ref[q * share + pair * 2 * columns : q * share + (pair + 1) * 2 * columns, :]
                for q in range(cuts)
            ],
            axis=0,
        )
        back = dot_nt(weight, mix_grad).reshape(cuts, 2 * columns, batch)
        term = local[pair * 2 * columns : (pair + 1) * 2 * columns]
        back = back + jnp.where(q_index == own, term[None], 0.0)
        at = pair * batch
        turned_s[:, at : at + batch] = back[:, :columns].reshape(lanes, batch).astype(jnp.bfloat16)
        turned_s[:, half + at : half + at + batch] = back[:, columns:].reshape(lanes, batch).astype(jnp.bfloat16)
    slot_grad = dot(turned_s[...], count_ref[...]).T
    parts = swap_blocks([slot_grad[j * owners : (j + 1) * owners] for j in range(cap)], columns)
    for q in range(cuts):
        grad_ref[q] = parts[q].astype(jnp.bfloat16)


def call(kernel, out_shape, in_spaces, scratch=(), limit=48, out_space=pltpu.VMEM, **kw):
    outs = jax.tree.map(lambda unused: pl.BlockSpec(memory_space=out_space), out_shape)
    return pl.pallas_call(
        kernel,
        out_shape=out_shape,
        in_specs=[pl.BlockSpec(memory_space=space) for space in in_spaces],
        out_specs=outs,
        scratch_shapes=list(scratch),
        compiler_params=pltpu.CompilerParams(vmem_limit_bytes=limit * 2**20),
        **kw,
    )


def pick(ids, emb, shards, lanes, **kw):
    scratch = [
        pltpu.VMEM(ids.shape, ids.dtype),
        pltpu.VMEM(emb.shape, emb.dtype),
        pltpu.SemaphoreType.DMA,
        pltpu.SemaphoreType.DMA,
    ]
    out = jax.ShapeDtypeStruct((shards, 1, lanes), jnp.bfloat16)
    return call(pick_kernel, out, [pltpu.HBM, pltpu.HBM], scratch, limit=62, **kw)(ids, emb)


def scatter(ids, grads, rows_out, **kw):
    V = pltpu.VMEM
    return call(scatter_kernel, jax.ShapeDtypeStruct((rows_out, LANES), jnp.float32), [V, V], limit=16, **kw)(ids, grads)


def count(slot, bag, cap, tables, bags, slots, side, **kw):
    V, S = pltpu.VMEM, pltpu.SMEM
    width = slots // 2
    out = jax.ShapeDtypeStruct((bags, width), jnp.int8)
    pitch = tables + 1
    rows = (bags // tables - 1) * pitch + tables + window_rows(tables, pitch)
    rows = (rows + 7) // 8 * 8
    return call(
        functools.partial(count_kernel, cap, slots // cap, tables, pitch, side * width),
        out,
        [S, V, V],
        [
            pltpu.VMEM((width // LANES, rows, LANES), jnp.float32),
            pltpu.VMEM(out.shape, out.dtype),
            pltpu.SemaphoreType.DMA((8,)),
        ],
        out_space=pltpu.HBM,
        limit=58,
        **kw,
    )(bag, slot, bag)


def cross(own, low, high, rows, weight, bias, up, cap, **kw):
    V, S = pltpu.VMEM, pltpu.SMEM
    cuts, owners, lanes = rows.shape
    bags, width = low.shape
    return call(
        functools.partial(cross_kernel, cap),
        (jax.ShapeDtypeStruct(up.shape, jnp.bfloat16), jax.ShapeDtypeStruct(rows.shape, jnp.bfloat16)),
        [S, pltpu.HBM, pltpu.HBM, V, pltpu.HBM, V, V],
        [
            pltpu.VMEM((2, bags, width), low.dtype),
            pltpu.VMEM((bags, 2 * width), jnp.bfloat16),
            pltpu.VMEM(weight.shape, weight.dtype),
            pltpu.VMEM((bags // 2, 2 * lanes), jnp.bfloat16),
            pltpu.VMEM((lanes, bags), jnp.bfloat16),
            pltpu.SemaphoreType.DMA((8,)),
            pltpu.SemaphoreType.DMA,
        ],
        limit=50,
        **kw,
    )(own, low, high, rows, weight, bias, up)


def per_device(embedding, cross_weight, cross_bias, upstream, unique_rows, lookup_slot, bag_of_lookup):
    owners = lax.axis_size("table")
    cuts = lax.axis_size("cuts")
    rows_dev, columns = embedding.shape
    cap = unique_rows.shape[2]
    batch, share = upstream.shape
    tables = share // columns
    lanes = cap * columns
    highs = rows_dev // LANES
    ids = unique_rows[:, 0, :].T
    emb = embedding.T.reshape(columns, highs, LANES).transpose(1, 0, 2).reshape(highs * columns, LANES)
    picked = pick(ids, emb, owners, lanes)
    arrived = lax.all_to_all(picked, "table", 0, 0, tiled=True)
    sizes = (cap, tables, batch * tables, owners * cap)
    low = count(lookup_slot, bag_of_lookup, *sizes, 0)
    arrived, low, lookup_slot, bag_of_lookup = lax.optimization_barrier(
        (arrived, low, lookup_slot, bag_of_lookup)
    )
    rows = lax.all_to_all(
        jnp.broadcast_to(arrived.reshape(1, owners, lanes), (cuts, owners, lanes)), "cuts", 0, 0, tiled=True
    )
    high = count(lookup_slot, bag_of_lookup, *sizes, 1)
    own = lax.axis_index("cuts").astype(jnp.int32).reshape(1)
    cross_out, grads = cross(
        own, low, high, rows, cross_weight, cross_bias.reshape(1, share), upstream, cap
    )
    grads = lax.all_to_all(grads, "cuts", 0, 0, tiled=True)
    grads = jnp.sum(grads.astype(jnp.float32), axis=0).astype(jnp.bfloat16)
    returned = lax.all_to_all(grads, "table", 0, 0, tiled=True)
    row_grads = scatter(ids, returned, highs * columns)
    row_grads = row_grads.reshape(highs, columns, LANES).transpose(1, 0, 2).reshape(columns, rows_dev).T
    return cross_out, row_grads


def solution(mesh):
    return jax.shard_map(
        per_device,
        mesh=mesh,
        in_specs=(
            P("table", "cuts"),
            P(None, "cuts"),
            P("cuts"),
            P("table", "cuts"),
            P(None, "table", None),
            P("table", None),
            P("table", None),
        ),
        out_specs=(P("table", "cuts"), P("table", "cuts")),
        check_vma=False,
    )
```
